256 devices in a mesh: sec: 8 (over x, y_lo), ta: 32 (over z, y_hi, core).
Axes of the slice: x: 4, y: 4 (y_hi: 2, y_lo: 2; y = y_hi * 2 + y_lo), z: 8, core: 2. Of those that a mesh axis runs over, the one named last changes fastest.
Arguments:
- sink_vectors: bfloat16 [2, 32, 8192, 512], P(None, 'ta', 'sec'), may hold values from -0.046875 to 0.046875
- propagators: bfloat16 [3, 2, 32, 8192, 512], P(None, None, 'ta', 'sec'), may hold values from -6 to 6
- live_rows: int32 [8], replicated, may hold values from 512 to 1024, as said below
- source_times: int32 [3], replicated, may hold values from 0 to 31
Outputs:
- sandwich: bfloat16 [3, 3, 3, 2, 32, 512, 512], P(None, None, None, None, 'ta', 'sec')
The draws below stay inside these ranges and needn't reach their ends.
Inputs may be any that keep to these rules, and one draw needn't show every extreme that they name: `live_rows`: some section has exactly 1024 live rows in every draw.
All inputs are finite; a program needn't handle non-finite values.
Results may differ from the reference program's by a relative error of at most 0.02.
Values may be sent and summed in bfloat16 or wider, within the bound.
A program may use at most 64 MiB of HBM per device.

```python
import jax
import jax.numpy as jnp
from jax import lax

ORDER = 512
SOURCES = 3
STOPS = 3
ROWS_DEV = 1024
SITES = 8192
TIMES = 32
N_SEC = 8


def draw_live_rows(key, part):
    counts = jax.random.randint(key, (N_SEC,), ROWS_DEV // 2, ROWS_DEV + 1)
    chosen = jax.random.randint(jax.random.fold_in(key, 7), (), 0, N_SEC)
    return counts.at[chosen].set(ROWS_DEV).astype(jnp.int32)


def levels(stream_key, dims, pieces, least, high):
    loudness = 1.0
    for dim, parts in pieces:
        heights = jax.random.uniform(jax.random.fold_in(jax.random.fold_in(stream_key, 6), dim), (parts,), jnp.float32, least / len(pieces), high / len(pieces))
        loudness = loudness * jnp.repeat(jnp.exp(heights), dims[dim] // parts).reshape((-1,) + (1,) * (len(dims) - 1 - dim))
    return loudness


def noise(own_key, extent, width, limit, cuts=(), kind=jnp.bfloat16):
    level = levels(own_key, extent, cuts, -0.22, 0.18) if cuts else 1.0
    values = jax.random.normal(own_key, extent, jnp.float32) * width * level
    return jnp.minimum(jnp.maximum(values, -limit), limit).astype(kind)


def setup_inputs(seed: int = 0) -> dict:
    key_of = jax.random.split(jax.random.key(seed), 5)
    return {
        "sink_vectors": noise(key_of[0], (2, TIMES, SITES, ORDER), (2 * SITES) ** -0.5, 0.046875, ((1, 32), (2, 8))),
        "propagators": noise(key_of[1], (SOURCES, 2, TIMES, SITES, ORDER), 1.0, 6.0, ((2, 32), (3, 8))),
        "live_rows": draw_live_rows(jax.random.fold_in(key_of[4], 71), 0),
        "source_times": jax.random.randint(key_of[3], (SOURCES,), 0, TIMES).astype(jnp.int32),
    }


def reference(sink_vectors, propagators, live_rows, source_times):
    live_mask = (jnp.arange(ROWS_DEV, dtype=jnp.int32)[None, :] < live_rows[:, None]).astype(jnp.bfloat16).reshape(-1)

    def meson_at(moment):
        sink_rows = lax.dynamic_index_in_dim(sink_vectors, moment, 1, keepdims=False) * live_mask[None, :, None]
        prop_rows = lax.dynamic_index_in_dim(propagators, moment, 2, keepdims=False)
        sink_split = sink_rows.reshape(2, N_SEC, ROWS_DEV, ORDER).astype(jnp.float32)
        prop_split = prop_rows.reshape(SOURCES, 2, N_SEC, ROWS_DEV, ORDER).astype(jnp.float32)
        products = jnp.einsum("cnrx,sdnry->nxscdy", sink_split, prop_split)
        real_part = products[:, :, :, 0, 0] + products[:, :, :, 1, 1]
        imag_part = products[:, :, :, 0, 1] - products[:, :, :, 1, 0]
        stacked = jnp.stack((real_part, imag_part), 3)
        sign_flip = jnp.where(moment < source_times, -1.0, 1.0).astype(jnp.float32)
        partial_low = (stacked * sign_flip[None, None, :, None, None]).astype(jnp.bfloat16)
        partial_low = lax.optimization_barrier(partial_low)
        return jnp.sum(partial_low.astype(jnp.float32), 0).astype(jnp.bfloat16)

    mesons = lax.map(meson_at, jnp.arange(TIMES, dtype=jnp.int32))
    scale_factor = 0.5 * ORDER ** -0.5

    def sandwich_at(pair):
        local_full, remote_full = pair
        products = jnp.einsum("iacx,xbdj->abcdij", local_full.astype(jnp.float32), remote_full.astype(jnp.float32))
        real_part = products[:, :, 0, 0] - products[:, :, 1, 1]
        imag_part = products[:, :, 0, 1] + products[:, :, 1, 0]
        return (jnp.stack((real_part, imag_part), 2) * scale_factor).astype(jnp.bfloat16)

    results = []
    for stop_index in range(STOPS):
        remote = jnp.roll(mesons, stop_index + 1, axis=0)
        results.append(lax.map(sandwich_at, (mesons, remote)))
    stacked_all = jnp.stack(results, 0)
    return jnp.transpose(stacked_all, (0, 2, 3, 4, 1, 5, 6))
```

```python
import functools

import jax
import jax.numpy as jnp
from jax import lax
from jax.experimental import pallas as pl
from jax.experimental.pallas import tpu as pltpu
from jax.sharding import PartitionSpec as P

MESH = pl.DeviceIdType.MESH
NX = 4
NSEC = 8
BF = jnp.bfloat16
F32 = jnp.float32


def kernel(
    n_ta,
    live_ref, times_ref, sink_hbm, prop_hbm, out_hbm,
    sink, prop, et, part, rx, ysend, yrecv, keep, mine, a2, bbuf, tbuf, outb,
    in_sem, out_sem, rx_send, rx_recv, y_send, y_recv,
    push_send, tpush_send, b_recv, t_recv, relay_send, relay2_send, core_send,
):
    order = sink.shape[2]
    rows = sink.shape[1]
    blk = order // NSEC
    wide = order // NX
    n_src = prop.shape[0]
    n_z = n_ta // 4

    sec = lax.axis_index("sec")
    ta = lax.axis_index("ta")
    x, ylo = sec // 2, sec % 2
    z, yhi, c = ta // 4, (ta // 2) % 2, ta % 2
    single = c == yhi

    def dev(xx, yl, zz, yh, cc):
        return (xx * 2 + yl, zz * 4 + yh * 2 + cc)

    def xoff(o):
        return (x + o) % NX

    partner = dev(x, 1 - ylo, z, yhi, c)
    across = dev(x, 1 - ylo, z, 1 - yhi, 1 - c)
    other = dev(x, ylo, z, yhi, 1 - c)

    barrier = pltpu.get_barrier_semaphore()
    greet = [dev(xoff(o), ylo, z, yhi, c) for o in (1, 2, 3)] + [partner, across]
    greet += [
        dev(xoff(o), ylo, (z + dz) % n_z, yhi, 1 - c) for o in range(NX) for dz in (0, 1, n_z - 1)
    ]
    for device in greet:
        pl.semaphore_signal(barrier, inc=1, device_id=device, device_id_type=MESH)

    loads = [pltpu.make_async_copy(sink_hbm, sink, in_sem.at[0])]
    loads += [
        pltpu.make_async_copy(prop_hbm.at[a], prop.at[a], in_sem.at[1 + a]) for a in range(n_src)
    ]
    for load in loads:
        load.start()

    loads[0].wait()
    alive = lax.broadcasted_iota(jnp.int32, (1, rows), 1) < live_ref[sec]
    for q in range(NX):
        re = sink[0, :, q * wide:(q + 1) * wide].T
        im = sink[1, :, q * wide:(q + 1) * wide].T
        zero = jnp.zeros_like(re)
        re = jnp.where(alive, re, zero)
        im = jnp.where(alive, im, zero)
        et[q, 0, :, 0:rows] = re
        et[q, 0, :, rows:2 * rows] = im
        et[q, 1, :, 0:rows] = -im
        et[q, 1, :, rows:2 * rows] = re

    def rx_copy(a, o):
        return pltpu.make_async_remote_copy(
            src_ref=part.at[a, xoff(o)], dst_ref=rx.at[a, 3 - o],
            send_sem=rx_send.at[a, o - 1], recv_sem=rx_recv.at[a, 3 - o],
            device_id=dev(xoff(o), ylo, z, yhi, c), device_id_type=MESH,
        )

    def multiply(a, send):
        loads[1 + a].wait()
        sign = jnp.where(ta < times_ref[a], -1.0, 1.0).astype(F32)
        for o in (2, 1, 3, 0):
            q = xoff(o)
            lhs = et[q].reshape(2 * wide, 2 * rows)
            rhs = prop[a].reshape(2 * rows, order)
            res = jnp.dot(lhs, rhs, preferred_element_type=F32) * sign
            part[a, q] = res.astype(BF).reshape(2, wide, order)
            if send and o:
                rx_copy(a, o).start()

    def scatter(a):
        for o in (2, 1, 3):
            rx_copy(a, o).start()

    def scatter_wait(a):
        for o in (2, 1, 3):
            rx_copy(a, o).wait_send()

    def y_copy(a):
        return pltpu.make_async_remote_copy(
            src_ref=ysend.at[a], dst_ref=yrecv.at[a],
            send_sem=y_send.at[a], recv_sem=y_recv.at[a],
            device_id=partner, device_id_type=MESH,
        )

    def sum_half(a, half):
        span = pl.ds(pl.multiple_of(half * blk, blk), blk)
        total = part[a, x, :, span, :].astype(F32)
        for k in range(3):
            total = total + rx[a, k, :, span, :].astype(F32)
        return total

    def stage_a(a):
        for k in range(3):
            rx_copy(a, 3 - k).wait_recv()
        ysend[a] = sum_half(a, 1 - ylo).astype(BF)
        y_copy(a).start()
        keep[a] = sum_half(a, ylo)

    def span_of(xx, yl):
        return pl.ds(pl.multiple_of((xx * 2 + yl) * blk, blk), blk)

    def block(p, a, xx, yl):
        return bbuf.at[p, a, :, span_of(xx, yl), :]

    def remote(src, dst, send, recv, device):
        return pltpu.make_async_remote_copy(
            src_ref=src, dst_ref=dst, send_sem=send, recv_sem=recv,
            device_id=device, device_id_type=MESH,
        )

    def push(a, o):
        return remote(
            mine.at[a], block(0, a, x, ylo), push_send.at[a, o], b_recv.at[0, a, sec],
            dev(xoff(o), ylo, (z + c) % n_z, yhi, 1 - c),
        )

    def tpush(a, o):
        return remote(
            mine.at[a], tbuf.at[a, x], tpush_send.at[a, o], t_recv.at[a, x],
            dev(xoff(o), ylo, (z + yhi) % n_z, yhi, 1 - c),
        )

    def move(p_from, p_to, a, xx, yl, sems, k, device):
        return remote(
            block(p_from, a, xx, yl), block(p_to, a, xx, yl),
            sems.at[a, k], b_recv.at[p_to, a, xx * 2 + yl], device,
        )

    def wait_block(p, a, xx, yl):
        move(p, p, a, xx, yl, core_send, 0, other).wait_recv()

    def t_across(a, o):
        return remote(
            tbuf.at[a, xoff(o)], block(2, a, xoff(o), ylo), relay2_send.at[a, o],
            b_recv.at[2, a, xoff(o) * 2 + ylo], across,
        )

    def gray(o):
        return o + o // 2 - 2 * (o // 3)

    def stage_b(a):
        y_copy(a).wait_recv()
        total = (keep[a] + yrecv[a].astype(F32)).astype(BF)
        mine[a] = total
        re, im = total[0], total[1]
        a2[a, 0, :, 0:order] = re
        a2[a, 0, :, order:2 * order] = -im
        a2[a, 1, :, 0:order] = im
        a2[a, 1, :, order:2 * order] = re

        @pl.loop(0, NX)
        def _(i):
            push(a, gray(i)).start()

        @pl.when(jnp.logical_not(single))
        def _():
            @pl.loop(0, NX)
            def _(i):
                tpush(a, gray(i)).start()

    def stage_c(a):
        @pl.when(single)
        def _():
            @pl.loop(0, NX)
            def _(i):
                o = gray(i)
                remote(
                    mine.at[a], tbuf.at[a, xoff(o)], tpush_send.at[a, o],
                    t_recv.at[a, xoff(o)], other,
                ).wait_recv()
                t_across(a, o).start()
                wait_block(0, a, xoff(o), ylo)
                move(0, 0, a, xoff(o), ylo, relay_send, o, partner).start()

        @pl.when(jnp.logical_not(single))
        def _():
            @pl.loop(0, NX)
            def _(i):
                o = gray(i)
                wait_block(0, a, xoff(o), ylo)
                move(0, 0, a, xoff(o), ylo, relay_send, o, partner).start()
                move(0, 1, a, xoff(o), ylo, relay2_send, o, across).start()

    def stage_d(a):
        @pl.when(single)
        def _():
            @pl.loop(0, NX)
            def _(i):
                o = gray(i)
                wait_block(2, a, xoff(o), 1 - ylo)
                move(2, 2, a, xoff(o), 1 - ylo, relay_send, NX + o, partner).start()
                move(2, 2, a, xoff(o), 1 - ylo, core_send, o, other).start()

        @pl.when(jnp.logical_not(single))
        def _():
            @pl.loop(0, NX)
            def _(i):
                o = gray(i)
                wait_block(0, a, xoff(o), 1 - ylo)
                move(0, 1, a, xoff(o), 1 - ylo, relay_send, NX + o, across).start()
                wait_block(1, a, xoff(o), 1 - ylo)
                move(1, 1, a, xoff(o), 1 - ylo, core_send, o, other).start()

    def stage_e(a):
        @pl.when(single)
        def _():
            @pl.loop(0, NX)
            def _(i):
                o = gray(i)
                wait_block(2, a, xoff(o), ylo)
                move(2, 2, a, xoff(o), ylo, core_send, NX + o, other).start()

            @pl.loop(0, NX)
            def _(i):
                wait_block(0, a, xoff(gray(i)), 1 - ylo)

            @pl.loop(0, NSEC)
            def _(i):
                wait_block(1, a, i // 2, i % 2)

        @pl.when(jnp.logical_not(single))
        def _():
            @pl.loop(0, NX)
            def _(i):
                o = gray(i)
                wait_block(1, a, xoff(o), ylo)
                move(1, 1, a, xoff(o), ylo, core_send, NX + o, other).start()

            @pl.loop(0, NSEC)
            def _(i):
                wait_block(2, a, i // 2, i % 2)

    places = (2 * (1 - c), yhi + c, c + 1 - yhi)
    scale = 0.5 * order ** -0.5

    def out_copy(p, b):
        return pltpu.make_async_copy(
            outb.at[p, b], out_hbm.at[places[p], :, b], out_sem.at[p, b]
        )

    def stage_f(b):
        for p in range(3):
            lhs = a2[...].reshape(n_src * 2 * blk, 2 * order)
            rhs = bbuf[p, b].reshape(2 * order, order)
            res = jnp.dot(lhs, rhs, preferred_element_type=F32) * scale
            outb[p, b] = res.astype(BF).reshape(n_src, 2, blk, order)
            out_copy(p, b).start()

    multiply_first = True
    pl.semaphore_wait(barrier, len(greet))
    multiply(0, multiply_first)
    multiply(1, False)
    scatter_wait(0)
    scatter(1)
    stage_a(0)
    multiply(2, False)
    stage_b(0)
    scatter_wait(1)
    scatter(2)
    stage_c(0)
    stage_a(1)
    stage_d(0)
    stage_b(1)
    stage_c(1)
    stage_a(2)
    stage_b(2)
    stage_e(0)
    stage_d(1)
    stage_c(2)
    stage_f(0)
    stage_e(1)
    stage_d(2)
    stage_f(1)
    stage_e(2)
    stage_f(2)

    scatter_wait(2)
    for a in range(n_src):
        y_copy(a).wait_send()
        for p in range(3):
            out_copy(p, a).wait()

        @pl.loop(0, NX)
        def _(o):
            push(a, o).wait_send()
            move(0, 0, a, xoff(o), ylo, relay_send, o, partner).wait_send()
            move(0, 0, a, xoff(o), ylo, relay2_send, o, across).wait_send()
            move(0, 0, a, xoff(o), ylo, relay_send, NX + o, partner).wait_send()
            move(0, 0, a, xoff(o), ylo, core_send, o, other).wait_send()
            move(0, 0, a, xoff(o), ylo, core_send, NX + o, other).wait_send()

        @pl.when(jnp.logical_not(single))
        def _():
            @pl.loop(0, NX)
            def _(o):
                tpush(a, o).wait_send()


def fused(n_ta, sink, prop, live, times):
    n_src, _, rows, order = prop.shape
    blk, wide = order // NSEC, order // NX
    dma = pltpu.SemaphoreType.DMA
    return pl.pallas_call(
        functools.partial(kernel, n_ta),
        out_shape=jax.ShapeDtypeStruct((3, n_src, n_src, 2, blk, order), BF),
        in_specs=[pl.BlockSpec(memory_space=pltpu.SMEM)] * 2
        + [pl.BlockSpec(memory_space=pl.ANY)] * 2,
        out_specs=pl.BlockSpec(memory_space=pl.ANY),
        scratch_shapes=[
            pltpu.VMEM((2, rows, order), BF),
            pltpu.VMEM((n_src, 2, rows, order), BF),
            pltpu.VMEM((NX, 2, wide, 2 * rows), BF),
            pltpu.VMEM((n_src, NX, 2, wide, order), BF),
            pltpu.VMEM((n_src, 3, 2, wide, order), BF),
            pltpu.VMEM((n_src, 2, blk, order), BF),
            pltpu.VMEM((n_src, 2, blk, order), BF),
            pltpu.VMEM((n_src, 2, blk, order), F32),
            pltpu.VMEM((n_src, 2, blk, order), BF),
            pltpu.VMEM((n_src, 2, blk, 2 * order), BF),
            pltpu.VMEM((3, n_src, 2, order, order), BF),
            pltpu.VMEM((n_src, NX, 2, blk, order), BF),
            pltpu.VMEM((3, n_src, n_src, 2, blk, order), BF),
            dma((1 + n_src,)),
            dma((3, n_src)),
            dma((n_src, 3)),
            dma((n_src, 3)),
            dma((n_src,)),
            dma((n_src,)),
            dma((n_src, NX)),
            dma((n_src, NX)),
            dma((3, n_src, NSEC)),
            dma((n_src, NX)),
            dma((n_src, 2 * NX)),
            dma((n_src, NX)),
            dma((n_src, 2 * NX)),
        ],
        compiler_params=pltpu.CompilerParams(
            collective_id=0, has_side_effects=True, vmem_limit_bytes=56 * 1024 * 1024
        ),
        cost_estimate=pl.CostEstimate(
            flops=10_000_000_000, bytes_accessed=12_000_000, transcendentals=0
        ),
    )(live, times, sink, prop)


def solution(mesh):
    n_ta = mesh.shape["ta"]

    def local(sink_vectors, propagators, live_rows, source_times):
        res = fused(n_ta, sink_vectors[:, 0], propagators[:, :, 0], live_rows, source_times)
        return res[:, :, :, :, None]

    return jax.shard_map(
        local,
        mesh=mesh,
        in_specs=(P(None, "ta", "sec", None), P(None, None, "ta", "sec", None), P(), P()),
        out_specs=P(None, None, None, None, "ta", "sec", None),
        check_vma=False,
    )
```

```python
import functools

import jax
import jax.numpy as jnp
from jax import lax
from jax.experimental import pallas as pl
from jax.experimental.pallas import tpu as pltpu
from jax.sharding import PartitionSpec as P

MESH = pl.DeviceIdType.MESH
NX = 4
NSEC = 8
BF = jnp.bfloat16
F32 = jnp.float32


def kernel(
    n_ta,
    live_ref, times_ref, sink_hbm, prop_hbm, out_hbm,
    sink, prop, et, part, rfar, rnear, ysend, yrecv, keep, mine, a2, bbuf, tbuf, outb,
    in_sem, out_sem, far_send, far_recv, near_send, near_recv, y_send, y_recv,
    push_send, tpush_send, b_recv, t_recv, relay_send, relay2_send, core_send,
    row_send, row_recv, pair_send, pair_recv,
):
    order = sink.shape[2]
    rows = sink.shape[1]
    blk = order // NSEC
    wide = order // NX
    n_src = prop.shape[0]
    n_z = n_ta // 4

    sec = lax.axis_index("sec")
    ta = lax.axis_index("ta")
    x, ylo = sec // 2, sec % 2
    z, yhi, c = ta // 4, (ta // 2) % 2, ta % 2
    single = c == yhi

    def dev(xx, yl, zz, yh, cc):
        return (xx * 2 + yl, zz * 4 + yh * 2 + cc)

    def xoff(o):
        return (x + o) % NX

    partner = dev(x, 1 - ylo, z, yhi, c)
    across = dev(x, 1 - ylo, z, 1 - yhi, 1 - c)
    other = dev(x, ylo, z, yhi, 1 - c)

    barrier = pltpu.get_barrier_semaphore()
    greet = [dev(xoff(o), ylo, z, yhi, c) for o in (1, 3)] + [partner, across]
    greet += [
        dev(xoff(o), ylo, (z + dz) % n_z, yhi, 1 - c) for o in range(NX) for dz in (0, 1, n_z - 1)
    ]
    for device in greet:
        pl.semaphore_signal(barrier, inc=1, device_id=device, device_id_type=MESH)

    loads = [pltpu.make_async_copy(sink_hbm, sink, in_sem.at[0])]
    loads += [
        pltpu.make_async_copy(prop_hbm.at[a], prop.at[a], in_sem.at[1 + a]) for a in range(n_src)
    ]
    for load in loads:
        load.start()

    loads[0].wait()
    alive = lax.broadcasted_iota(jnp.int32, (1, rows), 1) < live_ref[sec]
    for q in range(NX):
        re = sink[0, :, q * wide:(q + 1) * wide].T
        im = sink[1, :, q * wide:(q + 1) * wide].T
        zero = jnp.zeros_like(re)
        re = jnp.where(alive, re, zero)
        im = jnp.where(alive, im, zero)
        et[q, 0, :, 0:rows] = re
        et[q, 0, :, rows:2 * rows] = im
        et[q, 1, :, 0:rows] = -im
        et[q, 1, :, rows:2 * rows] = re

    right, left = dev(xoff(1), ylo, z, yhi, c), dev(xoff(3), ylo, z, yhi, c)
    toward = (right, left)
    near = (xoff(1), xoff(3))
    halves = (pl.ds(0, blk), pl.ds(blk, blk))

    def remote(src, dst, send, recv, device):
        return pltpu.make_async_remote_copy(
            src_ref=src, dst_ref=dst, send_sem=send, recv_sem=recv,
            device_id=device, device_id_type=MESH,
        )

    def far_copy(a, d):
        return remote(
            part.at[a, xoff(2), :, halves[d], :], rfar.at[a, d],
            far_send.at[a, d], far_recv.at[a, d], toward[d],
        )

    def near_copy(a, d, h):
        return remote(
            part.at[a, near[d], :, halves[h], :], rnear.at[a, d, :, halves[h], :],
            near_send.at[a, d, h], near_recv.at[a, d, h], toward[d],
        )

    def multiply(a, send):
        loads[1 + a].wait()
        sign = jnp.where(ta < times_ref[a], -1.0, 1.0).astype(F32)
        for o in (2, 1, 3, 0):
            q = xoff(o)
            lhs = et[q].reshape(2 * wide, 2 * rows)
            rhs = prop[a].reshape(2 * rows, order)
            res = jnp.dot(lhs, rhs, preferred_element_type=F32) * sign
            part[a, q] = res.astype(BF).reshape(2, wide, order)
            if send and o == 2:
                far_copy(a, 0).start()
                far_copy(a, 1).start()
            if send and o in (1, 3):
                near_copy(a, o // 2, 1 - o // 2).start()

    def scatter(a):
        for d in range(2):
            far_copy(a, d).start()
        for d in range(2):
            near_copy(a, d, 1 - d).start()

    def stage_r(a):
        for d in range(2):
            far_copy(a, d).wait_recv()
            mid = part[a, near[d], :, halves[d], :].astype(F32) + rfar[a, d].astype(F32)
            part[a, near[d], :, halves[d], :] = mid.astype(BF)
            near_copy(a, d, d).start()

    def y_copy(a):
        return pltpu.make_async_remote_copy(
            src_ref=ysend.at[a], dst_ref=yrecv.at[a],
            send_sem=y_send.at[a], recv_sem=y_recv.at[a],
            device_id=partner, device_id_type=MESH,
        )

    def sum_half(a, half):
        span = pl.ds(pl.multiple_of(half * blk, blk), blk)
        total = part[a, x, :, span, :].astype(F32)
        for k in range(2):
            total = total + rnear[a, k, :, span, :].astype(F32)
        return total

    def stage_a(a):
        for d in range(2):
            for h in range(2):
                near_copy(a, d, h).wait_recv()
        ysend[a] = sum_half(a, 1 - ylo).astype(BF)
        y_copy(a).start()
        keep[a] = sum_half(a, ylo)

    def span_of(xx, yl):
        return pl.ds(pl.multiple_of((xx * 2 + yl) * blk, blk), blk)

    def block(p, a, xx, yl):
        return bbuf.at[p, a, :, span_of(xx, yl), :]

    def push(a, o):
        return remote(
            mine.at[a], block(0, a, x, ylo), push_send.at[a, o], b_recv.at[0, a, sec],
            dev(xoff(o), ylo, (z + c) % n_z, yhi, 1 - c),
        )

    def tpush(a, o):
        return remote(
            mine.at[a], tbuf.at[a, x], tpush_send.at[a, o], t_recv.at[a, x],
            dev(xoff(o), ylo, (z + yhi) % n_z, yhi, 1 - c),
        )

    def move(p_from, p_to, a, xx, yl, sems, k, device):
        return remote(
            block(p_from, a, xx, yl), block(p_to, a, xx, yl),
            sems.at[a, k], b_recv.at[p_to, a, xx * 2 + yl], device,
        )

    def wait_block(p, a, xx, yl):
        move(p, p, a, xx, yl, core_send, 0, other).wait_recv()

    def t_across(a, o):
        return remote(
            tbuf.at[a, xoff(o)], block(2, a, xoff(o), ylo), relay2_send.at[a, o],
            b_recv.at[2, a, xoff(o) * 2 + ylo], across,
        )

    def gray(o):
        return o + o // 2 - 2 * (o // 3)

    def each(count, step):
        if count == 1:
            step(0)
        else:
            pl.loop(0, count)(lambda i: step(gray(i)))

    def stage_b(a, count):
        y_copy(a).wait_recv()
        total = (keep[a] + yrecv[a].astype(F32)).astype(BF)
        mine[a] = total
        each(count, lambda o: push(a, o).start())

        @pl.when(jnp.logical_not(single))
        def _():
            each(count, lambda o: tpush(a, o).start())

        re, im = total[0], total[1]
        a2[a, 0, :, 0:order] = re
        a2[a, 0, :, order:2 * order] = -im
        a2[a, 1, :, 0:order] = im
        a2[a, 1, :, order:2 * order] = re

    def stage_c(a, count):
        @pl.when(single)
        def _():
            def step(o):
                remote(
                    mine.at[a], tbuf.at[a, xoff(o)], tpush_send.at[a, o],
                    t_recv.at[a, xoff(o)], other,
                ).wait_recv()
                t_across(a, o).start()
                wait_block(0, a, xoff(o), ylo)
                move(0, 0, a, xoff(o), ylo, relay_send, o, partner).start()

            each(count, step)

        @pl.when(jnp.logical_not(single))
        def _():
            def step(o):
                wait_block(0, a, xoff(o), ylo)
                move(0, 1, a, xoff(o), ylo, relay2_send, o, across).start()
                move(0, 0, a, xoff(o), ylo, relay_send, o, partner).start()

            each(count, step)

    def stage_d(a, count):
        @pl.when(single)
        def _():
            def step(o):
                wait_block(2, a, xoff(o), 1 - ylo)
                move(2, 2, a, xoff(o), 1 - ylo, relay_send, NX + o, partner).start()
                if count > 1:
                    move(2, 2, a, xoff(o), 1 - ylo, core_send, o, other).start()

            each(count, step)

        @pl.when(jnp.logical_not(single))
        def _():
            def step(o):
                wait_block(0, a, xoff(o), 1 - ylo)
                move(0, 1, a, xoff(o), 1 - ylo, relay_send, NX + o, across).start()
                if count > 1:
                    wait_block(1, a, xoff(o), 1 - ylo)
                    move(1, 1, a, xoff(o), 1 - ylo, core_send, o, other).start()

            each(count, step)

    def stage_e(a):
        @pl.when(single)
        def _():
            @pl.loop(0, NX)
            def _(i):
                o = gray(i)
                wait_block(2, a, xoff(o), ylo)
                move(2, 2, a, xoff(o), ylo, core_send, NX + o, other).start()

            @pl.loop(0, NX)
            def _(i):
                wait_block(0, a, xoff(gray(i)), 1 - ylo)

            @pl.loop(0, NSEC)
            def _(i):
                wait_block(1, a, i // 2, i % 2)

        @pl.when(jnp.logical_not(single))
        def _():
            @pl.loop(0, NX)
            def _(i):
                o = gray(i)
                wait_block(1, a, xoff(o), ylo)
                move(1, 1, a, xoff(o), ylo, core_send, NX + o, other).start()

            @pl.loop(0, NSEC)
            def _(i):
                wait_block(2, a, i // 2, i % 2)

    last = n_src - 1
    role = 2 - (c + yhi) % 2

    def quarter(p, xx):
        return bbuf.at[p, last, :, pl.ds(pl.multiple_of(xx * wide, wide), wide), :]

    def quarter_part(p, xx, ri):
        return bbuf.at[p, last, ri, pl.ds(pl.multiple_of(xx * wide, wide), wide), :]

    def row_copy(kind, d):
        p = role if kind else 0
        return remote(
            quarter(p, x), quarter(p, x), row_send.at[kind, d], row_recv.at[kind, d], toward[d]
        )

    def row_wait(kind, d):
        p = role if kind else 0
        remote(
            quarter(p, near[1 - d]), quarter(p, near[1 - d]),
            row_send.at[kind, d], row_recv.at[kind, d], toward[d],
        ).wait_recv()

    def row_relay(kind, d):
        p = role if kind else 0
        return remote(
            quarter_part(p, near[1 - d], d), quarter_part(p, near[1 - d], d),
            row_send.at[kind, 2 + d], row_recv.at[kind, 2 + d], toward[d],
        )

    def relay_wait(kind, d):
        p = role if kind else 0
        remote(
            quarter_part(p, xoff(2), d), quarter_part(p, xoff(2), d),
            row_send.at[kind, 2 + d], row_recv.at[kind, 2 + d], toward[d],
        ).wait_recv()

    def pair_copy(p, o):
        return remote(
            quarter(p, xoff(o)), quarter(p, xoff(o)), pair_send.at[o], pair_recv.at[o], other
        )

    def stage_g():
        @pl.when(single)
        def _():
            wait_block(0, last, x, 1 - ylo)
        for d in range(2):
            row_copy(0, d).start()

        @pl.when(jnp.logical_not(single))
        def _():
            wait_block(1, last, x, 1 - ylo)
        wait_block(role, last, x, ylo)
        for d in range(2):
            row_copy(1, d).start()
        pair_copy(role, 0).start()

    def stage_h():
        for kind in range(2):
            for d in range(2):
                row_wait(kind, d)
                row_relay(kind, d).start()
                if kind:
                    pair_copy(role, 3 - 2 * d).start()

    def stage_i():
        for kind in range(2):
            for d in range(2):
                relay_wait(kind, d)
        pair_copy(role, 2).start()

    def stage_j():
        for o in (0, 1, 3, 2):
            pair_copy(3 - role, o).wait_recv()

    places = (2 * (1 - c), yhi + c, c + 1 - yhi)
    scale = 0.5 * order ** -0.5

    def out_copy(p, b):
        return pltpu.make_async_copy(
            outb.at[p, b], out_hbm.at[places[p], :, b], out_sem.at[p, b]
        )

    def stage_f(b):
        for p in range(3):
            lhs = a2[...].reshape(n_src * 2 * blk, 2 * order)
            rhs = bbuf[p, b].reshape(2 * order, order)
            res = jnp.dot(lhs, rhs, preferred_element_type=F32) * scale
            outb[p, b] = res.astype(BF).reshape(n_src, 2, blk, order)
            out_copy(p, b).start()

    pl.semaphore_wait(barrier, len(greet))
    multiply(0, True)
    multiply(1, False)
    stage_r(0)
    scatter(1)
    stage_a(0)
    multiply(2, False)
    stage_r(1)
    stage_b(0, NX)
    scatter(2)
    stage_a(1)
    stage_c(0, NX)
    stage_r(2)
    stage_b(1, NX)
    stage_d(0, NX)
    stage_a(2)
    stage_c(1, NX)
    stage_b(2, 1)
    stage_e(0)
    stage_c(2, 1)
    stage_d(1, NX)
    stage_d(2, 1)
    stage_g()
    stage_e(1)
    stage_f(0)
    stage_h()
    stage_f(1)
    stage_i()
    stage_j()
    stage_f(2)

    for a in range(n_src):
        y_copy(a).wait_send()
        for p in range(3):
            out_copy(p, a).wait()
        for d in range(2):
            far_copy(a, d).wait_send()
            for h in range(2):
                near_copy(a, d, h).wait_send()

        def drain(o):
            push(a, o).wait_send()
            move(0, 0, a, xoff(o), ylo, relay_send, o, partner).wait_send()
            move(0, 0, a, xoff(o), ylo, relay2_send, o, across).wait_send()
            move(0, 0, a, xoff(o), ylo, relay_send, NX + o, partner).wait_send()
            if a < last:
                move(0, 0, a, xoff(o), ylo, core_send, o, other).wait_send()
                move(0, 0, a, xoff(o), ylo, core_send, NX + o, other).wait_send()

            @pl.when(jnp.logical_not(single))
            def _():
                tpush(a, o).wait_send()

        each(1 if a == last else NX, drain)
    for kind in range(2):
        for d in range(2):
            row_copy(kind, d).wait_send()
            row_relay(kind, d).wait_send()
    for o in range(NX):
        pair_copy(role, o).wait_send()


def fused(n_ta, sink, prop, live, times):
    n_src, _, rows, order = prop.shape
    blk, wide = order // NSEC, order // NX
    dma = pltpu.SemaphoreType.DMA
    return pl.pallas_call(
        functools.partial(kernel, n_ta),
        out_shape=jax.ShapeDtypeStruct((3, n_src, n_src, 2, blk, order), BF),
        in_specs=[pl.BlockSpec(memory_space=pltpu.SMEM)] * 2
        + [pl.BlockSpec(memory_space=pl.ANY)] * 2,
        out_specs=pl.BlockSpec(memory_space=pl.ANY),
        scratch_shapes=[
            pltpu.VMEM((2, rows, order), BF),
            pltpu.VMEM((n_src, 2, rows, order), BF),
            pltpu.VMEM((NX, 2, wide, 2 * rows), BF),
            pltpu.VMEM((n_src, NX, 2, wide, order), BF),
            pltpu.VMEM((n_src, 2, 2, blk, order), BF),
            pltpu.VMEM((n_src, 2, 2, wide, order), BF),
            pltpu.VMEM((n_src, 2, blk, order), BF),
            pltpu.VMEM((n_src, 2, blk, order), BF),
            pltpu.VMEM((n_src, 2, blk, order), F32),
            pltpu.VMEM((n_src, 2, blk, order), BF),
            pltpu.VMEM((n_src, 2, blk, 2 * order), BF),
            pltpu.VMEM((3, n_src, 2, order, order), BF),
            pltpu.VMEM((n_src, NX, 2, blk, order), BF),
            pltpu.VMEM((3, n_src, n_src, 2, blk, order), BF),
            dma((1 + n_src,)),
            dma((3, n_src)),
            dma((n_src, 2)),
            dma((n_src, 2)),
            dma((n_src, 2, 2)),
            dma((n_src, 2, 2)),
            dma((n_src,)),
            dma((n_src,)),
            dma((n_src, NX)),
            dma((n_src, NX)),
            dma((3, n_src, NSEC)),
            dma((n_src, NX)),
            dma((n_src, 2 * NX)),
            dma((n_src, NX)),
            dma((n_src, 2 * NX)),
            dma((2, 4)),
            dma((2, 4)),
            dma((NX,)),
            dma((NX,)),
        ],
        compiler_params=pltpu.CompilerParams(
            collective_id=0, has_side_effects=True, vmem_limit_bytes=56 * 1024 * 1024
        ),
        cost_estimate=pl.CostEstimate(
            flops=10_000_000_000, bytes_accessed=12_000_000, transcendentals=0
        ),
    )(live, times, sink, prop)


def solution(mesh):
    n_ta = mesh.shape["ta"]

    def local(sink_vectors, propagators, live_rows, source_times):
        res = fused(n_ta, sink_vectors[:, 0], propagators[:, :, 0], live_rows, source_times)
        return res[:, :, :, :, None]

    return jax.shard_map(
        local,
        mesh=mesh,
        in_specs=(P(None, "ta", "sec", None), P(None, None, "ta", "sec", None), P(), P()),
        out_specs=P(None, None, None, None, "ta", "sec", None),
        check_vma=False,
    )
```

```python
import functools

import jax
import jax.numpy as jnp
from jax import lax
from jax.experimental import pallas as pl
from jax.experimental.pallas import tpu as pltpu
from jax.sharding import PartitionSpec as P

MESH = pl.DeviceIdType.MESH
NX = 4
NSEC = 8
BF = jnp.bfloat16
F32 = jnp.float32


def kernel(
    n_ta,
    live_ref, times_ref, sink_hbm, prop_hbm, out_hbm,
    sink, prop, et, part, rfar, rnear, ysend, yrecv, keep, mine, a2, bbuf, tbuf, outb,
    in_sem, out_sem, far_send, far_recv, near_send, near_recv, y_send, y_recv,
    push_send, tpush_send, b_recv, t_recv, relay_send, relay2_send, core_send,
    row_send, row_recv, pair_send, pair_recv,
):
    order = sink.shape[2]
    rows = sink.shape[1]
    blk = order // NSEC
    wide = order // NX
    n_src = prop.shape[0]
    n_z = n_ta // 4

    sec = lax.axis_index("sec")
    ta = lax.axis_index("ta")
    x, ylo = sec // 2, sec % 2
    z, yhi, c = ta // 4, (ta // 2) % 2, ta % 2
    single = c == yhi

    def dev(xx, yl, zz, yh, cc):
        return (xx * 2 + yl, zz * 4 + yh * 2 + cc)

    def xoff(o):
        return (x + o) % NX

    partner = dev(x, 1 - ylo, z, yhi, c)
    across = dev(x, 1 - ylo, z, 1 - yhi, 1 - c)
    other = dev(x, ylo, z, yhi, 1 - c)

    barrier = pltpu.get_barrier_semaphore()
    greet = [dev(xoff(o), ylo, z, yhi, c) for o in (1, 3)] + [partner, across]
    greet += [
        dev(xoff(o), ylo, (z + dz) % n_z, yhi, 1 - c) for o in range(NX) for dz in (0, 1, n_z - 1)
    ]
    for device in greet:
        pl.semaphore_signal(barrier, inc=1, device_id=device, device_id_type=MESH)

    loads = [pltpu.make_async_copy(sink_hbm, sink, in_sem.at[0])]
    loads += [
        pltpu.make_async_copy(prop_hbm.at[a], prop.at[a], in_sem.at[1 + a]) for a in range(n_src)
    ]
    loads[0].start()
    loads[1].start()

    def transpose(q):
        alive = lax.broadcasted_iota(jnp.int32, (1, rows), 1) < live_ref[sec]
        columns = pl.ds(pl.multiple_of(q * wide, wide), wide)
        re = sink[0, :, columns].T
        im = sink[1, :, columns].T
        zero = jnp.zeros_like(re)
        re = jnp.where(alive, re, zero)
        im = jnp.where(alive, im, zero)
        et[q, 0, :, 0:rows] = re
        et[q, 0, :, rows:2 * rows] = im
        et[q, 1, :, 0:rows] = -im
        et[q, 1, :, rows:2 * rows] = re

    right, left = dev(xoff(1), ylo, z, yhi, c), dev(xoff(3), ylo, z, yhi, c)
    toward = (right, left)
    near = (xoff(1), xoff(3))
    halves = (pl.ds(0, blk), pl.ds(blk, blk))

    def remote(src, dst, send, recv, device):
        return pltpu.make_async_remote_copy(
            src_ref=src, dst_ref=dst, send_sem=send, recv_sem=recv,
            device_id=device, device_id_type=MESH,
        )

    def far_copy(a, d):
        return remote(
            part.at[a, xoff(2), :, halves[d], :], rfar.at[a, d],
            far_send.at[a, d], far_recv.at[a, d], toward[d],
        )

    def near_copy(a, d, h):
        return remote(
            part.at[a, near[d], :, halves[h], :], rnear.at[a, d, :, halves[h], :],
            near_send.at[a, d, h], near_recv.at[a, d, h], toward[d],
        )

    def multiply(a, send):
        if a == 0:
            loads[0].wait()
            for load in loads[2:]:
                load.start()
        else:
            loads[1 + a].wait()
        sign = jnp.where(ta < times_ref[a], -1.0, 1.0).astype(F32)
        for o in (2, 1, 3, 0):
            q = xoff(o)
            if a == 0:
                transpose(q)
                if o == 2:
                    loads[1].wait()
            lhs = et[q].reshape(2 * wide, 2 * rows)
            rhs = prop[a].reshape(2 * rows, order)
            res = jnp.dot(lhs, rhs, preferred_element_type=F32) * sign
            part[a, q] = res.astype(BF).reshape(2, wide, order)
            if a == 0 and o == 2:
                pl.semaphore_wait(barrier, len(greet))
            if send and o == 2:
                far_copy(a, 0).start()
                far_copy(a, 1).start()
            if send and o in (1, 3):
                near_copy(a, o // 2, 1 - o // 2).start()
            if a == 0 and o == 3:
                stage_r(0)

    def scatter(a):
        for d in range(2):
            far_copy(a, d).start()
        for d in range(2):
            near_copy(a, d, 1 - d).start()

    def stage_r(a):
        for d in range(2):
            far_copy(a, d).wait_recv()
            mid = part[a, near[d], :, halves[d], :].astype(F32) + rfar[a, d].astype(F32)
            part[a, near[d], :, halves[d], :] = mid.astype(BF)
            near_copy(a, d, d).start()

    def y_copy(a):
        return pltpu.make_async_remote_copy(
            src_ref=ysend.at[a], dst_ref=yrecv.at[a],
            send_sem=y_send.at[a], recv_sem=y_recv.at[a],
            device_id=partner, device_id_type=MESH,
        )

    def sum_half(a, half):
        span = pl.ds(pl.multiple_of(half * blk, blk), blk)
        total = part[a, x, :, span, :].astype(F32)
        for k in range(2):
            total = total + rnear[a, k, :, span, :].astype(F32)
        return total

    def stage_a(a):
        for d in range(2):
            for h in range(2):
                near_copy(a, d, h).wait_recv()
        ysend[a] = sum_half(a, 1 - ylo).astype(BF)
        y_copy(a).start()
        keep[a] = sum_half(a, ylo)

    def span_of(xx, yl):
        return pl.ds(pl.multiple_of((xx * 2 + yl) * blk, blk), blk)

    def block(p, a, xx, yl):
        return bbuf.at[p, a, :, span_of(xx, yl), :]

    def push(a, o):
        return remote(
            mine.at[a], block(0, a, x, ylo), push_send.at[a, o], b_recv.at[0, a, sec],
            dev(xoff(o), ylo, (z + c) % n_z, yhi, 1 - c),
        )

    def tpush(a, o):
        return remote(
            mine.at[a], tbuf.at[a, x], tpush_send.at[a, o], t_recv.at[a, x],
            dev(xoff(o), ylo, (z + yhi) % n_z, yhi, 1 - c),
        )

    def move(p_from, p_to, a, xx, yl, sems, k, device):
        return remote(
            block(p_from, a, xx, yl), block(p_to, a, xx, yl),
            sems.at[a, k], b_recv.at[p_to, a, xx * 2 + yl], device,
        )

    def wait_block(p, a, xx, yl):
        move(p, p, a, xx, yl, core_send, 0, other).wait_recv()

    def t_across(a, o):
        return remote(
            tbuf.at[a, xoff(o)], block(2, a, xoff(o), ylo), relay2_send.at[a, o],
            b_recv.at[2, a, xoff(o) * 2 + ylo], across,
        )

    order_x = (0, 1, 3, 2)
    yfirst = 0
    role = 2 - (c + yhi) % 2

    def stage_b(a, offsets):
        y_copy(a).wait_recv()
        total = (keep[a] + yrecv[a].astype(F32)).astype(BF)
        mine[a] = total
        for o in offsets:
            push(a, o).start()

        @pl.when(jnp.logical_not(single))
        def _():
            for o in offsets:
                tpush(a, o).start()

        re, im = total[0], total[1]
        a2[a, 0, :, 0:order] = re
        a2[a, 0, :, order:2 * order] = -im
        a2[a, 1, :, 0:order] = im
        a2[a, 1, :, order:2 * order] = re

    def stage_c(a, offsets):
        @pl.when(single)
        def _():
            for o in offsets:
                remote(
                    mine.at[a], tbuf.at[a, xoff(o)], tpush_send.at[a, o],
                    t_recv.at[a, xoff(o)], other,
                ).wait_recv()
                t_across(a, o).start()
                wait_block(0, a, xoff(o), ylo)
                move(0, 0, a, xoff(o), ylo, relay_send, o, partner).start()

        @pl.when(jnp.logical_not(single))
        def _():
            for o in offsets:
                wait_block(0, a, xoff(o), ylo)
                move(0, 1, a, xoff(o), ylo, relay2_send, o, across).start()
                move(0, 0, a, xoff(o), ylo, relay_send, o, partner).start()

    def stage_d(a, offsets):
        @pl.when(single)
        def _():
            for o in offsets:
                wait_block(2, a, xoff(o), 1 - ylo)
                move(2, 2, a, xoff(o), 1 - ylo, relay_send, NX + o, partner).start()
                if a != yfirst:
                    move(2, 2, a, xoff(o), 1 - ylo, core_send, o, other).start()

        @pl.when(jnp.logical_not(single))
        def _():
            for o in offsets:
                wait_block(0, a, xoff(o), 1 - ylo)
                move(0, 1, a, xoff(o), 1 - ylo, relay_send, NX + o, across).start()
                if a != yfirst:
                    wait_block(1, a, xoff(o), 1 - ylo)
                    move(1, 1, a, xoff(o), 1 - ylo, core_send, o, other).start()

    def stage_e(a):
        for o in order_x:
            wait_block(role, a, xoff(o), ylo)
            move(role, role, a, xoff(o), ylo, core_send, NX + o, other).start()

    def stage_ew(a):
        @pl.when(single)
        def _():
            for o in range(NX):
                wait_block(0, a, o, 1 - ylo)
        for i in range(NSEC):
            wait_block(3 - role, a, i // 2, i % 2)


    def quarter(p, xx):
        return bbuf.at[p, yfirst, :, pl.ds(pl.multiple_of(xx * wide, wide), wide), :]

    def quarter_part(p, xx, ri):
        return bbuf.at[p, yfirst, ri, pl.ds(pl.multiple_of(xx * wide, wide), wide), :]

    def row_copy(kind, d):
        p = role if kind else 0
        return remote(
            quarter(p, x), quarter(p, x), row_send.at[kind, d], row_recv.at[kind, d], toward[d]
        )

    def row_wait(kind, d):
        p = role if kind else 0
        remote(
            quarter(p, near[1 - d]), quarter(p, near[1 - d]),
            row_send.at[kind, d], row_recv.at[kind, d], toward[d],
        ).wait_recv()

    def row_relay(kind, d):
        p = role if kind else 0
        return remote(
            quarter_part(p, near[1 - d], d), quarter_part(p, near[1 - d], d),
            row_send.at[kind, 2 + d], row_recv.at[kind, 2 + d], toward[d],
        )

    def relay_wait(kind, d):
        p = role if kind else 0
        remote(
            quarter_part(p, xoff(2), d), quarter_part(p, xoff(2), d),
            row_send.at[kind, 2 + d], row_recv.at[kind, 2 + d], toward[d],
        ).wait_recv()

    def pair_copy(p, o):
        return remote(
            quarter(p, xoff(o)), quarter(p, xoff(o)), pair_send.at[o], pair_recv.at[o], other
        )

    def stage_g():
        @pl.when(single)
        def _():
            wait_block(0, yfirst, x, 1 - ylo)
        for d in range(2):
            row_copy(0, d).start()

    def stage_gr():
        @pl.when(jnp.logical_not(single))
        def _():
            wait_block(1, yfirst, x, 1 - ylo)
        wait_block(role, yfirst, x, ylo)
        for d in range(2):
            row_copy(1, d).start()
        pair_copy(role, 0).start()

    def stage_h(kind):
        for d in range(2):
            row_wait(kind, d)
            row_relay(kind, d).start()
            if kind:
                pair_copy(role, 3 - 2 * d).start()

    def stage_i():
        for kind in range(2):
            for d in range(2):
                relay_wait(kind, d)
        pair_copy(role, 2).start()

    def stage_j():
        for o in order_x:
            pair_copy(3 - role, o).wait_recv()

    places = (2 * (1 - c), yhi + c, c + 1 - yhi)
    scale = 0.5 * order ** -0.5

    def out_copy(p, b):
        return pltpu.make_async_copy(
            outb.at[p, b], out_hbm.at[places[p], :, b], out_sem.at[p, b]
        )

    def stage_f(b):
        for p in range(3):
            lhs = a2[...].reshape(n_src * 2 * blk, 2 * order)
            rhs = bbuf[p, b].reshape(2 * order, order)
            res = jnp.dot(lhs, rhs, preferred_element_type=F32) * scale
            outb[p, b] = res.astype(BF).reshape(n_src, 2, blk, order)
            out_copy(p, b).start()

    multiply(0, True)
    multiply(1, True)
    stage_a(0)
    multiply(2, False)
    stage_r(1)
    scatter(2)
    stage_b(0, (0,))
    stage_a(1)
    stage_c(0, (0,))
    stage_r(2)
    stage_b(1, order_x)
    stage_d(0, (0,))
    stage_a(2)
    stage_c(1, (0,))
    stage_b(2, order_x)
    stage_g()
    stage_c(1, (1, 3))
    stage_c(2, (0,))
    stage_c(1, (2,))
    stage_gr()
    stage_d(1, (0, 1))
    stage_c(2, (1, 3))
    stage_d(1, (3, 2))
    stage_h(0)
    stage_c(2, (2,))
    stage_h(1)
    stage_d(2, (0, 1))
    stage_e(1)
    stage_d(2, (3, 2))
    stage_ew(1)
    stage_i()
    stage_f(1)
    stage_e(2)
    stage_j()
    stage_f(0)
    stage_ew(2)
    stage_f(2)

    for a in range(n_src):
        y_copy(a).wait_send()
        for p in range(3):
            out_copy(p, a).wait()
        for d in range(2):
            far_copy(a, d).wait_send()
            for h in range(2):
                near_copy(a, d, h).wait_send()

        def drain(o):
            push(a, o).wait_send()
            move(0, 0, a, xoff(o), ylo, relay_send, o, partner).wait_send()
            move(0, 0, a, xoff(o), ylo, relay2_send, o, across).wait_send()
            move(0, 0, a, xoff(o), ylo, relay_send, NX + o, partner).wait_send()
            if a != yfirst:
                move(0, 0, a, xoff(o), ylo, core_send, o, other).wait_send()
                move(0, 0, a, xoff(o), ylo, core_send, NX + o, other).wait_send()

            @pl.when(jnp.logical_not(single))
            def _():
                tpush(a, o).wait_send()

        for o in range(1 if a == yfirst else NX):
            drain(o)
    for kind in range(2):
        for d in range(2):
            row_copy(kind, d).wait_send()
            row_relay(kind, d).wait_send()
    for o in range(NX):
        pair_copy(role, o).wait_send()


def fused(n_ta, sink, prop, live, times):
    n_src, _, rows, order = prop.shape
    blk, wide = order // NSEC, order // NX
    dma = pltpu.SemaphoreType.DMA
    return pl.pallas_call(
        functools.partial(kernel, n_ta),
        out_shape=jax.ShapeDtypeStruct((3, n_src, n_src, 2, blk, order), BF),
        in_specs=[pl.BlockSpec(memory_space=pltpu.SMEM)] * 2
        + [pl.BlockSpec(memory_space=pl.ANY)] * 2,
        out_specs=pl.BlockSpec(memory_space=pl.ANY),
        scratch_shapes=[
            pltpu.VMEM((2, rows, order), BF),
            pltpu.VMEM((n_src, 2, rows, order), BF),
            pltpu.VMEM((NX, 2, wide, 2 * rows), BF),
            pltpu.VMEM((n_src, NX, 2, wide, order), BF),
            pltpu.VMEM((n_src, 2, 2, blk, order), BF),
            pltpu.VMEM((n_src, 2, 2, wide, order), BF),
            pltpu.VMEM((n_src, 2, blk, order), BF),
            pltpu.VMEM((n_src, 2, blk, order), BF),
            pltpu.VMEM((n_src, 2, blk, order), F32),
            pltpu.VMEM((n_src, 2, blk, order), BF),
            pltpu.VMEM((n_src, 2, blk, 2 * order), BF),
            pltpu.VMEM((3, n_src, 2, order, order), BF),
            pltpu.VMEM((n_src, NX, 2, blk, order), BF),
            pltpu.VMEM((3, n_src, n_src, 2, blk, order), BF),
            dma((1 + n_src,)),
            dma((3, n_src)),
            dma((n_src, 2)),
            dma((n_src, 2)),
            dma((n_src, 2, 2)),
            dma((n_src, 2, 2)),
            dma((n_src,)),
            dma((n_src,)),
            dma((n_src, NX)),
            dma((n_src, NX)),
            dma((3, n_src, NSEC)),
            dma((n_src, NX)),
            dma((n_src, 2 * NX)),
            dma((n_src, NX)),
            dma((n_src, 2 * NX)),
            dma((2, 4)),
            dma((2, 4)),
            dma((NX,)),
            dma((NX,)),
        ],
        compiler_params=pltpu.CompilerParams(
            collective_id=0, has_side_effects=True, vmem_limit_bytes=56 * 1024 * 1024
        ),
        cost_estimate=pl.CostEstimate(
            flops=10_000_000_000, bytes_accessed=12_000_000, transcendentals=0
        ),
    )(live, times, sink, prop)


def solution(mesh):
    n_ta = mesh.shape["ta"]

    def local(sink_vectors, propagators, live_rows, source_times):
        res = fused(n_ta, sink_vectors[:, 0], propagators[:, :, 0], live_rows, source_times)
        return res[:, :, :, :, None]

    return jax.shard_map(
        local,
        mesh=mesh,
        in_specs=(P(None, "ta", "sec", None), P(None, None, "ta", "sec", None), P(), P()),
        out_specs=P(None, None, None, None, "ta", "sec", None),
        check_vma=False,
    )
```

```python
import functools

import jax
import jax.numpy as jnp
from jax import lax
from jax.experimental import pallas as pl
from jax.experimental.pallas import tpu as pltpu
from jax.sharding import PartitionSpec as P

MESH = pl.DeviceIdType.MESH
NX = 4
NSEC = 8
BF = jnp.bfloat16
F32 = jnp.float32


def kernel(
    n_ta,
    live_ref, times_ref, sink_hbm, prop_hbm, out_hbm,
    sink, prop, et, part, rfar, rnear, ysend, yrecv, keep, mine, a2, bbuf, tbuf, outb,
    in_sem, out_sem, far_send, far_recv, near_send, near_recv, y_send, y_recv,
    push_send, tpush_send, b_recv, t_recv, relay_send, relay2_send, core_send,
    row_send, row_recv, pair_send, pair_recv,
):
    order = sink.shape[2]
    rows = sink.shape[1]
    blk = order // NSEC
    wide = order // NX
    n_src = prop.shape[0]
    n_z = n_ta // 4

    sec = lax.axis_index("sec")
    ta = lax.axis_index("ta")
    x, ylo = sec // 2, sec % 2
    z, yhi, c = ta // 4, (ta // 2) % 2, ta % 2
    single = c == yhi

    def dev(xx, yl, zz, yh, cc):
        return (xx * 2 + yl, zz * 4 + yh * 2 + cc)

    def xoff(o):
        return (x + o) % NX

    partner = dev(x, 1 - ylo, z, yhi, c)
    across = dev(x, 1 - ylo, z, 1 - yhi, 1 - c)
    other = dev(x, ylo, z, yhi, 1 - c)

    barrier = pltpu.get_barrier_semaphore()
    greet = [dev(xoff(o), ylo, z, yhi, c) for o in (1, 3)] + [partner, across]
    greet += [
        dev(xoff(o), ylo, (z + dz) % n_z, yhi, 1 - c) for o in range(NX) for dz in (0, 1, n_z - 1)
    ]
    for device in greet:
        pl.semaphore_signal(barrier, inc=1, device_id=device, device_id_type=MESH)

    loads = [pltpu.make_async_copy(sink_hbm, sink, in_sem.at[0])]
    loads += [
        pltpu.make_async_copy(prop_hbm.at[a], prop.at[a], in_sem.at[1 + a]) for a in range(n_src)
    ]
    loads[0].start()
    loads[1].start()

    def transpose(q):
        alive = lax.broadcasted_iota(jnp.int32, (1, rows), 1) < live_ref[sec]
        columns = pl.ds(pl.multiple_of(q * wide, wide), wide)
        re = sink[0, :, columns].T
        im = sink[1, :, columns].T
        zero = jnp.zeros_like(re)
        re = jnp.where(alive, re, zero)
        im = jnp.where(alive, im, zero)
        et[q, 0, :, 0:rows] = re
        et[q, 0, :, rows:2 * rows] = im
        et[q, 1, :, 0:rows] = -im
        et[q, 1, :, rows:2 * rows] = re

    right, left = dev(xoff(1), ylo, z, yhi, c), dev(xoff(3), ylo, z, yhi, c)
    toward = (right, left)
    near = (xoff(1), xoff(3))
    halves = (pl.ds(0, blk), pl.ds(blk, blk))

    def remote(src, dst, send, recv, device):
        return pltpu.make_async_remote_copy(
            src_ref=src, dst_ref=dst, send_sem=send, recv_sem=recv,
            device_id=device, device_id_type=MESH,
        )

    def far_copy(a, d):
        return remote(
            part.at[a, xoff(2), :, halves[d], :], rfar.at[a, d],
            far_send.at[a, d], far_recv.at[a, d], toward[d],
        )

    def near_copy(a, d, h):
        return remote(
            part.at[a, near[d], :, halves[h], :], rnear.at[a, d, :, halves[h], :],
            near_send.at[a, d, h], near_recv.at[a, d, h], toward[d],
        )

    def multiply(a, send):
        if a == 0:
            loads[0].wait()
            for load in loads[2:]:
                load.start()
        else:
            loads[1 + a].wait()
        sign = jnp.where(ta < times_ref[a], -1.0, 1.0).astype(F32)
        for o in (2, 1, 3, 0):
            q = xoff(o)
            if a == 0:
                transpose(q)
                if o == 2:
                    loads[1].wait()
            lhs = et[q].reshape(2 * wide, 2 * rows)
            rhs = prop[a].reshape(2 * rows, order)
            res = jnp.dot(lhs, rhs, preferred_element_type=F32) * sign
            part[a, q] = res.astype(BF).reshape(2, wide, order)
            if a == 0 and o == 2:
                pl.semaphore_wait(barrier, len(greet))
            if send and o == 2:
                far_copy(a, 0).start()
                far_copy(a, 1).start()
            if send and o in (1, 3):
                near_copy(a, o // 2, 1 - o // 2).start()
            if a == 0 and o == 3:
                stage_r(0)

    def scatter(a):
        for d in range(2):
            far_copy(a, d).start()
        for d in range(2):
            near_copy(a, d, 1 - d).start()

    def stage_r(a):
        for d in range(2):
            far_copy(a, d).wait_recv()
            mid = part[a, near[d], :, halves[d], :].astype(F32) + rfar[a, d].astype(F32)
            part[a, near[d], :, halves[d], :] = mid.astype(BF)
            near_copy(a, d, d).start()

    def y_copy(a):
        return pltpu.make_async_remote_copy(
            src_ref=ysend.at[a], dst_ref=yrecv.at[a],
            send_sem=y_send.at[a], recv_sem=y_recv.at[a],
            device_id=partner, device_id_type=MESH,
        )

    def sum_half(a, half):
        span = pl.ds(pl.multiple_of(half * blk, blk), blk)
        total = part[a, x, :, span, :].astype(F32)
        for k in range(2):
            total = total + rnear[a, k, :, span, :].astype(F32)
        return total

    def stage_a(a):
        for d in range(2):
            for h in range(2):
                near_copy(a, d, h).wait_recv()
        ysend[a] = sum_half(a, 1 - ylo).astype(BF)
        y_copy(a).start()
        keep[a] = sum_half(a, ylo)

    def span_of(xx, yl):
        return pl.ds(pl.multiple_of((xx * 2 + yl) * blk, blk), blk)

    def block(p, a, xx, yl):
        return bbuf.at[p, a, :, span_of(xx, yl), :]

    def push(a, o):
        return remote(
            mine.at[a], block(0, a, x, ylo), push_send.at[a, o], b_recv.at[0, a, sec],
            dev(xoff(o), ylo, (z + c) % n_z, yhi, 1 - c),
        )

    def tpush(a, o):
        return remote(
            mine.at[a], tbuf.at[a, x], tpush_send.at[a, o], t_recv.at[a, x],
            dev(xoff(o), ylo, (z + yhi) % n_z, yhi, 1 - c),
        )

    def move(p_from, p_to, a, xx, yl, sems, k, device):
        return remote(
            block(p_from, a, xx, yl), block(p_to, a, xx, yl),
            sems.at[a, k], b_recv.at[p_to, a, xx * 2 + yl], device,
        )

    def wait_block(p, a, xx, yl):
        move(p, p, a, xx, yl, core_send, 0, other).wait_recv()

    def t_across(a, o):
        return remote(
            tbuf.at[a, xoff(o)], block(2, a, xoff(o), ylo), relay2_send.at[a, o],
            b_recv.at[2, a, xoff(o) * 2 + ylo], across,
        )

    order_x = (0, 1, 3, 2)
    yfirst = 0
    role = 2 - (c + yhi) % 2

    def stage_b(a, offsets):
        y_copy(a).wait_recv()
        total = (keep[a] + yrecv[a].astype(F32)).astype(BF)
        mine[a] = total
        for o in offsets:
            push(a, o).start()

        @pl.when(jnp.logical_not(single))
        def _():
            for o in offsets:
                tpush(a, o).start()

        re, im = total[0], total[1]
        a2[a, 0, :, 0:order] = re
        a2[a, 0, :, order:2 * order] = -im
        a2[a, 1, :, 0:order] = im
        a2[a, 1, :, order:2 * order] = re

    def stage_c(a, offsets):
        @pl.when(single)
        def _():
            for o in offsets:
                remote(
                    mine.at[a], tbuf.at[a, xoff(o)], tpush_send.at[a, o],
                    t_recv.at[a, xoff(o)], other,
                ).wait_recv()
                t_across(a, o).start()
                wait_block(0, a, xoff(o), ylo)
                move(0, 0, a, xoff(o), ylo, relay_send, o, partner).start()

        @pl.when(jnp.logical_not(single))
        def _():
            for o in offsets:
                wait_block(0, a, xoff(o), ylo)
                move(0, 1, a, xoff(o), ylo, relay2_send, o, across).start()
                move(0, 0, a, xoff(o), ylo, relay_send, o, partner).start()

    def stage_d(a, offsets):
        @pl.when(single)
        def _():
            for o in offsets:
                wait_block(2, a, xoff(o), 1 - ylo)
                move(2, 2, a, xoff(o), 1 - ylo, relay_send, NX + o, partner).start()
                if a != yfirst:
                    move(2, 2, a, xoff(o), 1 - ylo, core_send, o, other).start()

        @pl.when(jnp.logical_not(single))
        def _():
            for o in offsets:
                wait_block(0, a, xoff(o), 1 - ylo)
                move(0, 1, a, xoff(o), 1 - ylo, relay_send, NX + o, across).start()
                if a != yfirst:
                    wait_block(1, a, xoff(o), 1 - ylo)
                    move(1, 1, a, xoff(o), 1 - ylo, core_send, o, other).start()

    def stage_e(a):
        for o in order_x:
            wait_block(role, a, xoff(o), ylo)
            move(role, role, a, xoff(o), ylo, core_send, NX + o, other).start()

    def stage_ep(a):
        @pl.when(single)
        def _():
            for o in range(NX):
                wait_block(0, a, o, 1 - ylo)

    def stage_ew(a):
        for i in range(NSEC):
            wait_block(3 - role, a, i // 2, i % 2)


    def quarter(p, xx):
        return bbuf.at[p, yfirst, :, pl.ds(pl.multiple_of(xx * wide, wide), wide), :]

    def quarter_part(p, xx, ri):
        return bbuf.at[p, yfirst, ri, pl.ds(pl.multiple_of(xx * wide, wide), wide), :]

    def row_copy(kind, d):
        p = role if kind else 0
        return remote(
            quarter(p, x), quarter(p, x), row_send.at[kind, d], row_recv.at[kind, d], toward[d]
        )

    def row_wait(kind, d):
        p = role if kind else 0
        remote(
            quarter(p, near[1 - d]), quarter(p, near[1 - d]),
            row_send.at[kind, d], row_recv.at[kind, d], toward[d],
        ).wait_recv()

    def row_relay(kind, d):
        p = role if kind else 0
        return remote(
            quarter_part(p, near[1 - d], d), quarter_part(p, near[1 - d], d),
            row_send.at[kind, 2 + d], row_recv.at[kind, 2 + d], toward[d],
        )

    def relay_wait(kind, d):
        p = role if kind else 0
        remote(
            quarter_part(p, xoff(2), d), quarter_part(p, xoff(2), d),
            row_send.at[kind, 2 + d], row_recv.at[kind, 2 + d], toward[d],
        ).wait_recv()

    def pair_copy(p, o):
        return remote(
            quarter(p, xoff(o)), quarter(p, xoff(o)), pair_send.at[o], pair_recv.at[o], other
        )

    def stage_g():
        @pl.when(single)
        def _():
            wait_block(0, yfirst, x, 1 - ylo)
        for d in range(2):
            row_copy(0, d).start()

    def stage_gr():
        @pl.when(jnp.logical_not(single))
        def _():
            wait_block(1, yfirst, x, 1 - ylo)
        wait_block(role, yfirst, x, ylo)
        for d in range(2):
            row_copy(1, d).start()
        pair_copy(role, 0).start()

    def stage_h(kind):
        for d in range(2):
            row_wait(kind, d)
            row_relay(kind, d).start()
            if kind:
                pair_copy(role, 3 - 2 * d).start()

    def stage_i():
        for kind in range(2):
            for d in range(2):
                relay_wait(kind, d)
        pair_copy(role, 2).start()

    def stage_j():
        for o in order_x:
            pair_copy(3 - role, o).wait_recv()

    places = (2 * (1 - c), 1, 2 * c)
    sets = (0, role, 3 - role)
    scale = 0.5 * order ** -0.5

    def out_copy(p, b):
        return pltpu.make_async_copy(
            outb.at[p, b], out_hbm.at[places[p], :, b], out_sem.at[p, b]
        )

    def product(p, b):
        lhs = a2[...].reshape(n_src * 2 * blk, 2 * order)
        rhs = bbuf[sets[p], b].reshape(2 * order, order)
        res = jnp.dot(lhs, rhs, preferred_element_type=F32) * scale
        outb[p, b] = res.astype(BF).reshape(n_src, 2, blk, order)
        out_copy(p, b).start()

    def stage_f(b):
        for p in range(3):
            product(p, b)

    multiply(0, True)
    multiply(1, True)
    stage_a(0)
    multiply(2, False)
    stage_r(1)
    scatter(2)
    stage_b(0, (0,))
    stage_a(1)
    stage_c(0, (0,))
    stage_r(2)
    stage_b(1, order_x)
    stage_d(0, (0,))
    stage_a(2)
    stage_c(1, (0,))
    stage_b(2, order_x)
    stage_g()
    stage_d(1, (0,))
    stage_c(1, (1, 3))
    stage_c(2, (0,))
    stage_d(1, (1,))
    stage_c(1, (2,))
    stage_gr()
    stage_d(1, (3,))
    stage_c(2, (1, 3))
    stage_d(1, (2,))
    stage_d(2, (0,))
    stage_h(0)
    stage_c(2, (2,))
    stage_d(2, (1,))
    stage_h(1)
    stage_e(1)
    stage_d(2, (3, 2))
    stage_ep(1)
    stage_ew(1)
    stage_i()
    stage_f(1)
    stage_e(2)
    stage_ep(2)
    product(0, 2)
    product(1, 2)
    stage_j()
    stage_f(0)
    stage_ew(2)
    product(2, 2)

    for a in range(n_src):
        y_copy(a).wait_send()
        for p in range(3):
            out_copy(p, a).wait()
        for d in range(2):
            far_copy(a, d).wait_send()
            for h in range(2):
                near_copy(a, d, h).wait_send()

        def drain(o):
            push(a, o).wait_send()
            move(0, 0, a, xoff(o), ylo, relay_send, o, partner).wait_send()
            move(0, 0, a, xoff(o), ylo, relay2_send, o, across).wait_send()
            move(0, 0, a, xoff(o), ylo, relay_send, NX + o, partner).wait_send()
            if a != yfirst:
                move(0, 0, a, xoff(o), ylo, core_send, o, other).wait_send()
                move(0, 0, a, xoff(o), ylo, core_send, NX + o, other).wait_send()

            @pl.when(jnp.logical_not(single))
            def _():
                tpush(a, o).wait_send()

        for o in range(1 if a == yfirst else NX):
            drain(o)
    for kind in range(2):
        for d in range(2):
            row_copy(kind, d).wait_send()
            row_relay(kind, d).wait_send()
    for o in range(NX):
        pair_copy(role, o).wait_send()


def fused(n_ta, sink, prop, live, times):
    n_src, _, rows, order = prop.shape
    blk, wide = order // NSEC, order // NX
    dma = pltpu.SemaphoreType.DMA
    return pl.pallas_call(
        functools.partial(kernel, n_ta),
        out_shape=jax.ShapeDtypeStruct((3, n_src, n_src, 2, blk, order), BF),
        in_specs=[pl.BlockSpec(memory_space=pltpu.SMEM)] * 2
        + [pl.BlockSpec(memory_space=pl.ANY)] * 2,
        out_specs=pl.BlockSpec(memory_space=pl.ANY),
        scratch_shapes=[
            pltpu.VMEM((2, rows, order), BF),
            pltpu.VMEM((n_src, 2, rows, order), BF),
            pltpu.VMEM((NX, 2, wide, 2 * rows), BF),
            pltpu.VMEM((n_src, NX, 2, wide, order), BF),
            pltpu.VMEM((n_src, 2, 2, blk, order), BF),
            pltpu.VMEM((n_src, 2, 2, wide, order), BF),
            pltpu.VMEM((n_src, 2, blk, order), BF),
            pltpu.VMEM((n_src, 2, blk, order), BF),
            pltpu.VMEM((n_src, 2, blk, order), F32),
            pltpu.VMEM((n_src, 2, blk, order), BF),
            pltpu.VMEM((n_src, 2, blk, 2 * order), BF),
            pltpu.VMEM((3, n_src, 2, order, order), BF),
            pltpu.VMEM((n_src, NX, 2, blk, order), BF),
            pltpu.VMEM((3, n_src, n_src, 2, blk, order), BF),
            dma((1 + n_src,)),
            dma((3, n_src)),
            dma((n_src, 2)),
            dma((n_src, 2)),
            dma((n_src, 2, 2)),
            dma((n_src, 2, 2)),
            dma((n_src,)),
            dma((n_src,)),
            dma((n_src, NX)),
            dma((n_src, NX)),
            dma((3, n_src, NSEC)),
            dma((n_src, NX)),
            dma((n_src, 2 * NX)),
            dma((n_src, NX)),
            dma((n_src, 2 * NX)),
            dma((2, 4)),
            dma((2, 4)),
            dma((NX,)),
            dma((NX,)),
        ],
        compiler_params=pltpu.CompilerParams(
            collective_id=0, has_side_effects=True, vmem_limit_bytes=56 * 1024 * 1024
        ),
        cost_estimate=pl.CostEstimate(
            flops=10_000_000_000, bytes_accessed=12_000_000, transcendentals=0
        ),
    )(live, times, sink, prop)


def solution(mesh):
    n_ta = mesh.shape["ta"]

    def local(sink_vectors, propagators, live_rows, source_times):
        res = fused(n_ta, sink_vectors[:, 0], propagators[:, :, 0], live_rows, source_times)
        return res[:, :, :, :, None]

    return jax.shard_map(
        local,
        mesh=mesh,
        in_specs=(P(None, "ta", "sec", None), P(None, None, "ta", "sec", None), P(), P()),
        out_specs=P(None, None, None, None, "ta", "sec", None),
        check_vma=False,
    )
```

```python
import functools

import jax
import jax.numpy as jnp
from jax import lax
from jax.experimental import pallas as pl
from jax.experimental.pallas import tpu as pltpu
from jax.sharding import PartitionSpec as P

MESH = pl.DeviceIdType.MESH
NX = 4
NSEC = 8
BF = jnp.bfloat16
F32 = jnp.float32


def kernel(
    n_ta,
    live_ref, times_ref, sink_hbm, prop_hbm, out_hbm,
    sink, prop, et, part, rfar, rnear, ysend, yrecv, keep, mine, a2, bbuf, tbuf, outb,
    in_sem, out_sem, far_send, far_recv, near_send, near_recv, y_send, y_recv,
    push_send, tpush_send, b_recv, t_recv, relay_send, relay2_send, core_send,
    row_send, row_recv, pair_send, pair_recv,
):
    order = sink.shape[2]
    rows = sink.shape[1]
    blk = order // NSEC
    wide = order // NX
    n_src = prop.shape[0]
    n_z = n_ta // 4

    sec = lax.axis_index("sec")
    ta = lax.axis_index("ta")
    x, ylo = sec // 2, sec % 2
    z, yhi, c = ta // 4, (ta // 2) % 2, ta % 2
    single = c == yhi

    def dev(xx, yl, zz, yh, cc):
        return (xx * 2 + yl, zz * 4 + yh * 2 + cc)

    def xoff(o):
        return (x + o) % NX

    partner = dev(x, 1 - ylo, z, yhi, c)
    across = dev(x, 1 - ylo, z, 1 - yhi, 1 - c)
    other = dev(x, ylo, z, yhi, 1 - c)

    barrier = pltpu.get_barrier_semaphore()
    greet = [dev(xoff(o), ylo, z, yhi, c) for o in (1, 3)] + [partner, across]
    greet += [
        dev(xoff(o), ylo, (z + dz) % n_z, yhi, 1 - c) for o in range(NX) for dz in (0, 1, n_z - 1)
    ]
    for device in greet:
        pl.semaphore_signal(barrier, inc=1, device_id=device, device_id_type=MESH)

    loads = [pltpu.make_async_copy(sink_hbm, sink, in_sem.at[0])]
    loads += [
        pltpu.make_async_copy(prop_hbm.at[a], prop.at[a], in_sem.at[1 + a]) for a in range(n_src)
    ]
    loads[0].start()
    loads[1].start()

    def transpose(q):
        alive = lax.broadcasted_iota(jnp.int32, (1, rows), 1) < live_ref[sec]
        columns = pl.ds(pl.multiple_of(q * wide, wide), wide)
        re = sink[0, :, columns].T
        im = sink[1, :, columns].T
        zero = jnp.zeros_like(re)
        re = jnp.where(alive, re, zero)
        im = jnp.where(alive, im, zero)
        et[q, 0, :, 0:rows] = re
        et[q, 0, :, rows:2 * rows] = im
        et[q, 1, :, 0:rows] = -im
        et[q, 1, :, rows:2 * rows] = re

    right, left = dev(xoff(1), ylo, z, yhi, c), dev(xoff(3), ylo, z, yhi, c)
    toward = (right, left)
    near = (xoff(1), xoff(3))
    halves = (pl.ds(0, blk), pl.ds(blk, blk))

    def remote(src, dst, send, recv, device):
        return pltpu.make_async_remote_copy(
            src_ref=src, dst_ref=dst, send_sem=send, recv_sem=recv,
            device_id=device, device_id_type=MESH,
        )

    def far_copy(a, d):
        return remote(
            part.at[a, xoff(2), :, halves[d], :], rfar.at[a, d],
            far_send.at[a, d], far_recv.at[a, d], toward[d],
        )

    def near_copy(a, d, h):
        return remote(
            part.at[a, near[d], :, halves[h], :], rnear.at[a, d, :, halves[h], :],
            near_send.at[a, d, h], near_recv.at[a, d, h], toward[d],
        )

    def multiply(a, offsets):
        if a == 0 and 2 in offsets:
            loads[0].wait()
            for load in loads[2:]:
                load.start()
        elif 2 in offsets:
            loads[1 + a].wait()
        sign = jnp.where(ta < times_ref[a], -1.0, 1.0).astype(F32)
        for o in offsets:
            q = xoff(o)
            if a == 0:
                transpose(q)
                if o == 2:
                    loads[1].wait()
            lhs = et[q].reshape(2 * wide, 2 * rows)
            rhs = prop[a].reshape(2 * rows, order)
            res = jnp.dot(lhs, rhs, preferred_element_type=F32) * sign
            part[a, q] = res.astype(BF).reshape(2, wide, order)
            if a == 0 and o == 2:
                pl.semaphore_wait(barrier, len(greet))
            if o == 2:
                far_copy(a, 0).start()
                far_copy(a, 1).start()
            if o in (1, 3):
                near_copy(a, o // 2, 1 - o // 2).start()
            if a == 0 and o == 3:
                stage_r(0)

    def stage_r(a):
        for d in range(2):
            far_copy(a, d).wait_recv()
            mid = part[a, near[d], :, halves[d], :].astype(F32) + rfar[a, d].astype(F32)
            part[a, near[d], :, halves[d], :] = mid.astype(BF)
            near_copy(a, d, d).start()

    def y_copy(a):
        return pltpu.make_async_remote_copy(
            src_ref=ysend.at[a], dst_ref=yrecv.at[a],
            send_sem=y_send.at[a], recv_sem=y_recv.at[a],
            device_id=partner, device_id_type=MESH,
        )

    def sum_half(a, half):
        span = pl.ds(pl.multiple_of(half * blk, blk), blk)
        total = part[a, x, :, span, :].astype(F32)
        for k in range(2):
            total = total + rnear[a, k, :, span, :].astype(F32)
        return total

    def stage_a(a):
        for d in range(2):
            for h in range(2):
                near_copy(a, d, h).wait_recv()
        ysend[a] = sum_half(a, 1 - ylo).astype(BF)
        y_copy(a).start()
        keep[a] = sum_half(a, ylo)

    def span_of(xx, yl):
        return pl.ds(pl.multiple_of((xx * 2 + yl) * blk, blk), blk)

    def block(p, a, xx, yl):
        return bbuf.at[p, a, :, span_of(xx, yl), :]

    def push(a, o):
        return remote(
            mine.at[a], block(0, a, x, ylo), push_send.at[a, o], b_recv.at[0, a, sec],
            dev(xoff(o), ylo, (z + c) % n_z, yhi, 1 - c),
        )

    def tpush(a, o):
        return remote(
            mine.at[a], tbuf.at[a, x], tpush_send.at[a, o], t_recv.at[a, x],
            dev(xoff(o), ylo, (z + yhi) % n_z, yhi, 1 - c),
        )

    def move(p_from, p_to, a, xx, yl, sems, k, device):
        return remote(
            block(p_from, a, xx, yl), block(p_to, a, xx, yl),
            sems.at[a, k], b_recv.at[p_to, a, xx * 2 + yl], device,
        )

    def wait_block(p, a, xx, yl):
        move(p, p, a, xx, yl, core_send, 0, other).wait_recv()

    def t_across(a, o):
        return remote(
            tbuf.at[a, xoff(o)], block(2, a, xoff(o), ylo), relay2_send.at[a, o],
            b_recv.at[2, a, xoff(o) * 2 + ylo], across,
        )

    order_x = (0, 1, 3, 2)
    yfirst = 0
    role = 2 - (c + yhi) % 2

    def stage_b(a, offsets):
        y_copy(a).wait_recv()
        total = (keep[a] + yrecv[a].astype(F32)).astype(BF)
        mine[a] = total
        for o in offsets:
            push(a, o).start()

        @pl.when(jnp.logical_not(single))
        def _():
            for o in offsets:
                tpush(a, o).start()

        re, im = total[0], total[1]
        a2[a, 0, :, 0:order] = re
        a2[a, 0, :, order:2 * order] = -im
        a2[a, 1, :, 0:order] = im
        a2[a, 1, :, order:2 * order] = re

    def stage_c(a, offsets):
        @pl.when(single)
        def _():
            for o in offsets:
                remote(
                    mine.at[a], tbuf.at[a, xoff(o)], tpush_send.at[a, o],
                    t_recv.at[a, xoff(o)], other,
                ).wait_recv()
                t_across(a, o).start()
                wait_block(0, a, xoff(o), ylo)
                move(0, 0, a, xoff(o), ylo, relay_send, o, partner).start()

        @pl.when(jnp.logical_not(single))
        def _():
            for o in offsets:
                wait_block(0, a, xoff(o), ylo)
                move(0, 1, a, xoff(o), ylo, relay2_send, o, across).start()
                move(0, 0, a, xoff(o), ylo, relay_send, o, partner).start()

    def stage_d(a, offsets):
        @pl.when(single)
        def _():
            for o in offsets:
                wait_block(2, a, xoff(o), 1 - ylo)
                move(2, 2, a, xoff(o), 1 - ylo, relay_send, NX + o, partner).start()
                if a != yfirst:
                    move(2, 2, a, xoff(o), 1 - ylo, core_send, o, other).start()

        @pl.when(jnp.logical_not(single))
        def _():
            for o in offsets:
                wait_block(0, a, xoff(o), 1 - ylo)
                move(0, 1, a, xoff(o), 1 - ylo, relay_send, NX + o, across).start()
                if a != yfirst:
                    wait_block(1, a, xoff(o), 1 - ylo)
                    move(1, 1, a, xoff(o), 1 - ylo, core_send, o, other).start()

    def stage_e(a):
        for o in order_x:
            wait_block(role, a, xoff(o), ylo)
            move(role, role, a, xoff(o), ylo, core_send, NX + o, other).start()

    def stage_ep(a):
        @pl.when(single)
        def _():
            for o in range(NX):
                wait_block(0, a, o, 1 - ylo)

    def stage_ew(a):
        for i in range(NSEC):
            wait_block(3 - role, a, i // 2, i % 2)


    def quarter(p, xx):
        return bbuf.at[p, yfirst, :, pl.ds(pl.multiple_of(xx * wide, wide), wide), :]

    def quarter_part(p, xx, ri):
        return bbuf.at[p, yfirst, ri, pl.ds(pl.multiple_of(xx * wide, wide), wide), :]

    def row_copy(kind, d):
        p = role if kind else 0
        return remote(
            quarter(p, x), quarter(p, x), row_send.at[kind, d], row_recv.at[kind, d], toward[d]
        )

    def row_wait(kind, d):
        p = role if kind else 0
        remote(
            quarter(p, near[1 - d]), quarter(p, near[1 - d]),
            row_send.at[kind, d], row_recv.at[kind, d], toward[d],
        ).wait_recv()

    def row_relay(kind, d):
        p = role if kind else 0
        return remote(
            quarter_part(p, near[1 - d], d), quarter_part(p, near[1 - d], d),
            row_send.at[kind, 2 + d], row_recv.at[kind, 2 + d], toward[d],
        )

    def relay_wait(kind, d):
        p = role if kind else 0
        remote(
            quarter_part(p, xoff(2), d), quarter_part(p, xoff(2), d),
            row_send.at[kind, 2 + d], row_recv.at[kind, 2 + d], toward[d],
        ).wait_recv()

    def pair_copy(p, o):
        return remote(
            quarter(p, xoff(o)), quarter(p, xoff(o)), pair_send.at[o], pair_recv.at[o], other
        )

    def stage_g():
        @pl.when(single)
        def _():
            wait_block(0, yfirst, x, 1 - ylo)
        for d in range(2):
            row_copy(0, d).start()

    def stage_gr():
        @pl.when(jnp.logical_not(single))
        def _():
            wait_block(1, yfirst, x, 1 - ylo)
        wait_block(role, yfirst, x, ylo)
        for d in range(2):
            row_copy(1, d).start()
        pair_copy(role, 0).start()

    def stage_h(kind):
        for d in range(2):
            row_wait(kind, d)
            row_relay(kind, d).start()
            if kind:
                pair_copy(role, 3 - 2 * d).start()

    def stage_i():
        for kind in range(2):
            for d in range(2):
                relay_wait(kind, d)
        pair_copy(role, 2).start()

    def stage_j():
        for o in order_x:
            pair_copy(3 - role, o).wait_recv()

    places = (2 * (1 - c), 1, 2 * c)
    sets = (0, role, 3 - role)
    scale = 0.5 * order ** -0.5

    def out_copy(p, b):
        return pltpu.make_async_copy(
            outb.at[p, b], out_hbm.at[places[p], :, b], out_sem.at[p, b]
        )

    def product(p, b):
        lhs = a2[...].reshape(n_src * 2 * blk, 2 * order)
        rhs = bbuf[sets[p], b].reshape(2 * order, order)
        res = jnp.dot(lhs, rhs, preferred_element_type=F32) * scale
        outb[p, b] = res.astype(BF).reshape(n_src, 2, blk, order)
        out_copy(p, b).start()

    def stage_f(b):
        for p in range(3):
            product(p, b)

    multiply(0, (2, 1, 3))
    multiply(1, (2, 1, 3))
    multiply(0, (0,))
    stage_a(0)
    multiply(1, (0,))
    stage_r(1)
    multiply(2, (2, 1, 3))
    stage_b(0, (0,))
    multiply(2, (0,))
    stage_a(1)
    stage_c(0, (0,))
    stage_r(2)
    stage_b(1, order_x)
    stage_d(0, (0,))
    stage_a(2)
    stage_c(1, (0,))
    stage_b(2, order_x)
    stage_g()
    stage_c(1, (1, 3))
    stage_c(2, (0,))
    stage_c(1, (2,))
    stage_gr()
    stage_d(1, (0, 1))
    stage_c(2, (1, 3))
    stage_d(1, (3, 2))
    stage_h(0)
    stage_c(2, (2,))
    stage_h(1)
    stage_d(2, (0, 1))
    stage_e(1)
    stage_d(2, (3, 2))
    stage_ep(1)
    stage_ew(1)
    stage_i()
    stage_f(1)
    stage_e(2)
    stage_ep(2)
    product(0, 2)
    product(1, 2)
    stage_j()
    stage_f(0)
    stage_ew(2)
    product(2, 2)

    for a in range(n_src):
        y_copy(a).wait_send()
        for p in range(3):
            out_copy(p, a).wait()
        for d in range(2):
            far_copy(a, d).wait_send()
            for h in range(2):
                near_copy(a, d, h).wait_send()

        def drain(o):
            push(a, o).wait_send()
            move(0, 0, a, xoff(o), ylo, relay_send, o, partner).wait_send()
            move(0, 0, a, xoff(o), ylo, relay2_send, o, across).wait_send()
            move(0, 0, a, xoff(o), ylo, relay_send, NX + o, partner).wait_send()
            if a != yfirst:
                move(0, 0, a, xoff(o), ylo, core_send, o, other).wait_send()
                move(0, 0, a, xoff(o), ylo, core_send, NX + o, other).wait_send()

            @pl.when(jnp.logical_not(single))
            def _():
                tpush(a, o).wait_send()

        for o in range(1 if a == yfirst else NX):
            drain(o)
    for kind in range(2):
        for d in range(2):
            row_copy(kind, d).wait_send()
            row_relay(kind, d).wait_send()
    for o in range(NX):
        pair_copy(role, o).wait_send()


def fused(n_ta, sink, prop, live, times):
    n_src, _, rows, order = prop.shape
    blk, wide = order // NSEC, order // NX
    dma = pltpu.SemaphoreType.DMA
    return pl.pallas_call(
        functools.partial(kernel, n_ta),
        out_shape=jax.ShapeDtypeStruct((3, n_src, n_src, 2, blk, order), BF),
        in_specs=[pl.BlockSpec(memory_space=pltpu.SMEM)] * 2
        + [pl.BlockSpec(memory_space=pl.ANY)] * 2,
        out_specs=pl.BlockSpec(memory_space=pl.ANY),
        scratch_shapes=[
            pltpu.VMEM((2, rows, order), BF),
            pltpu.VMEM((n_src, 2, rows, order), BF),
            pltpu.VMEM((NX, 2, wide, 2 * rows), BF),
            pltpu.VMEM((n_src, NX, 2, wide, order), BF),
            pltpu.VMEM((n_src, 2, 2, blk, order), BF),
            pltpu.VMEM((n_src, 2, 2, wide, order), BF),
            pltpu.VMEM((n_src, 2, blk, order), BF),
            pltpu.VMEM((n_src, 2, blk, order), BF),
            pltpu.VMEM((n_src, 2, blk, order), F32),
            pltpu.VMEM((n_src, 2, blk, order), BF),
            pltpu.VMEM((n_src, 2, blk, 2 * order), BF),
            pltpu.VMEM((3, n_src, 2, order, order), BF),
            pltpu.VMEM((n_src, NX, 2, blk, order), BF),
            pltpu.VMEM((3, n_src, n_src, 2, blk, order), BF),
            dma((1 + n_src,)),
            dma((3, n_src)),
            dma((n_src, 2)),
            dma((n_src, 2)),
            dma((n_src, 2, 2)),
            dma((n_src, 2, 2)),
            dma((n_src,)),
            dma((n_src,)),
            dma((n_src, NX)),
            dma((n_src, NX)),
            dma((3, n_src, NSEC)),
            dma((n_src, NX)),
            dma((n_src, 2 * NX)),
            dma((n_src, NX)),
            dma((n_src, 2 * NX)),
            dma((2, 4)),
            dma((2, 4)),
            dma((NX,)),
            dma((NX,)),
        ],
        compiler_params=pltpu.CompilerParams(
            collective_id=0, has_side_effects=True, vmem_limit_bytes=56 * 1024 * 1024
        ),
        cost_estimate=pl.CostEstimate(
            flops=10_000_000_000, bytes_accessed=12_000_000, transcendentals=0
        ),
    )(live, times, sink, prop)


def solution(mesh):
    n_ta = mesh.shape["ta"]

    def local(sink_vectors, propagators, live_rows, source_times):
        res = fused(n_ta, sink_vectors[:, 0], propagators[:, :, 0], live_rows, source_times)
        return res[:, :, :, :, None]

    return jax.shard_map(
        local,
        mesh=mesh,
        in_specs=(P(None, "ta", "sec", None), P(None, None, "ta", "sec", None), P(), P()),
        out_specs=P(None, None, None, None, "ta", "sec", None),
        check_vma=False,
    )
```

```python
import functools

import jax
import jax.numpy as jnp
from jax import lax
from jax.experimental import pallas as pl
from jax.experimental.pallas import tpu as pltpu
from jax.sharding import PartitionSpec as P

MESH = pl.DeviceIdType.MESH
NX = 4
NSEC = 8
BF = jnp.bfloat16
F32 = jnp.float32


def kernel(
    n_ta,
    live_ref, times_ref, sink_hbm, prop_hbm, out_hbm,
    sink, prop, et, part, rfar, rnear, ysend, yrecv, keep, mine, a2, bbuf, tbuf, outb,
    in_sem, out_sem, far_send, far_recv, near_send, near_recv, y_send, y_recv,
    push_send, tpush_send, b_recv, t_recv, relay_send, relay2_send, core_send,
    row_send, row_recv, pair_send, pair_recv,
):
    order = sink.shape[2]
    rows = sink.shape[1]
    blk = order // NSEC
    wide = order // NX
    n_src = prop.shape[0]
    n_z = n_ta // 4

    sec = lax.axis_index("sec")
    ta = lax.axis_index("ta")
    x, ylo = sec // 2, sec % 2
    z, yhi, c = ta // 4, (ta // 2) % 2, ta % 2
    single = c == yhi

    def dev(xx, yl, zz, yh, cc):
        return (xx * 2 + yl, zz * 4 + yh * 2 + cc)

    def xoff(o):
        return (x + o) % NX

    partner = dev(x, 1 - ylo, z, yhi, c)
    across = dev(x, 1 - ylo, z, 1 - yhi, 1 - c)
    other = dev(x, ylo, z, yhi, 1 - c)

    barrier = pltpu.get_barrier_semaphore()
    greet = [dev(xoff(o), ylo, z, yhi, c) for o in (1, 3)] + [partner, across]
    greet += [
        dev(xoff(o), ylo, (z + dz) % n_z, yhi, 1 - c) for o in range(NX) for dz in (0, 1, n_z - 1)
    ]
    for device in greet:
        pl.semaphore_signal(barrier, inc=1, device_id=device, device_id_type=MESH)

    loads = [pltpu.make_async_copy(sink_hbm, sink, in_sem.at[0])]
    loads += [
        pltpu.make_async_copy(prop_hbm.at[a], prop.at[a], in_sem.at[1 + a]) for a in range(n_src)
    ]
    loads[0].start()
    loads[1].start()

    def transpose(q):
        alive = lax.broadcasted_iota(jnp.int32, (1, rows), 1) < live_ref[sec]
        columns = pl.ds(pl.multiple_of(q * wide, wide), wide)
        re = sink[0, :, columns].T
        im = sink[1, :, columns].T
        zero = jnp.zeros_like(re)
        re = jnp.where(alive, re, zero)
        im = jnp.where(alive, im, zero)
        et[q, 0, :, 0:rows] = re
        et[q, 0, :, rows:2 * rows] = im
        et[q, 1, :, 0:rows] = -im
        et[q, 1, :, rows:2 * rows] = re

    right, left = dev(xoff(1), ylo, z, yhi, c), dev(xoff(3), ylo, z, yhi, c)
    toward = (right, left)
    near = (xoff(1), xoff(3))
    halves = (pl.ds(0, blk), pl.ds(blk, blk))

    def remote(src, dst, send, recv, device):
        return pltpu.make_async_remote_copy(
            src_ref=src, dst_ref=dst, send_sem=send, recv_sem=recv,
            device_id=device, device_id_type=MESH,
        )

    def far_copy(a, d):
        return remote(
            part.at[a, xoff(2), :, halves[d], :], rfar.at[a, d],
            far_send.at[a, d], far_recv.at[a, d], toward[d],
        )

    def near_copy(a, d, h):
        return remote(
            part.at[a, near[d], :, halves[h], :], rnear.at[a, d, :, halves[h], :],
            near_send.at[a, d, h], near_recv.at[a, d, h], toward[d],
        )

    def multiply(a, send):
        if a == 0:
            loads[0].wait()
            for load in loads[2:]:
                load.start()
        else:
            loads[1 + a].wait()
        sign = jnp.where(ta < times_ref[a], -1.0, 1.0).astype(F32)
        for o in (2, 1, 3, 0):
            q = xoff(o)
            if a == 0:
                transpose(q)
                if o == 2:
                    loads[1].wait()
            lhs = et[q].reshape(2 * wide, 2 * rows)
            rhs = prop[a].reshape(2 * rows, order)
            res = jnp.dot(lhs, rhs, preferred_element_type=F32) * sign
            part[a, q] = res.astype(BF).reshape(2, wide, order)
            if a == 0 and o == 2:
                pl.semaphore_wait(barrier, len(greet))
            if send and o == 2:
                far_copy(a, 0).start()
                far_copy(a, 1).start()
            if send and o in (1, 3):
                near_copy(a, o // 2, 1 - o // 2).start()
            if a == 0 and o == 3:
                stage_r(0)

    def scatter(a):
        for d in range(2):
            far_copy(a, d).start()
        for d in range(2):
            near_copy(a, d, 1 - d).start()

    def stage_r(a):
        for d in range(2):
            far_copy(a, d).wait_recv()
            mid = part[a, near[d], :, halves[d], :].astype(F32) + rfar[a, d].astype(F32)
            part[a, near[d], :, halves[d], :] = mid.astype(BF)
            near_copy(a, d, d).start()

    def y_copy(a):
        return pltpu.make_async_remote_copy(
            src_ref=ysend.at[a], dst_ref=yrecv.at[a],
            send_sem=y_send.at[a], recv_sem=y_recv.at[a],
            device_id=partner, device_id_type=MESH,
        )

    def sum_half(a, half):
        span = pl.ds(pl.multiple_of(half * blk, blk), blk)
        total = part[a, x, :, span, :].astype(F32)
        for k in range(2):
            total = total + rnear[a, k, :, span, :].astype(F32)
        return total

    def stage_a(a):
        for d in range(2):
            for h in range(2):
                near_copy(a, d, h).wait_recv()
        ysend[a] = sum_half(a, 1 - ylo).astype(BF)
        y_copy(a).start()
        keep[a] = sum_half(a, ylo)

    def span_of(xx, yl):
        return pl.ds(pl.multiple_of((xx * 2 + yl) * blk, blk), blk)

    def block(p, a, xx, yl):
        return bbuf.at[p, a, :, span_of(xx, yl), :]

    def push(a, o):
        return remote(
            mine.at[a], block(0, a, x, ylo), push_send.at[a, o], b_recv.at[0, a, sec],
            dev(xoff(o), ylo, (z + c) % n_z, yhi, 1 - c),
        )

    def tpush(a, o):
        return remote(
            mine.at[a], tbuf.at[a, x], tpush_send.at[a, o], t_recv.at[a, x],
            dev(xoff(o), ylo, (z + yhi) % n_z, yhi, 1 - c),
        )

    def move(p_from, p_to, a, xx, yl, sems, k, device):
        return remote(
            block(p_from, a, xx, yl), block(p_to, a, xx, yl),
            sems.at[a, k], b_recv.at[p_to, a, xx * 2 + yl], device,
        )

    def wait_block(p, a, xx, yl):
        move(p, p, a, xx, yl, core_send, 0, other).wait_recv()

    def t_across(a, o):
        return remote(
            tbuf.at[a, xoff(o)], block(2, a, xoff(o), ylo), relay2_send.at[a, o],
            b_recv.at[2, a, xoff(o) * 2 + ylo], across,
        )

    order_x = (0, 1, 3, 2)
    yfirst = 0
    role = 2 - (c + yhi) % 2

    def stage_b(a, offsets):
        y_copy(a).wait_recv()
        total = (keep[a] + yrecv[a].astype(F32)).astype(BF)
        mine[a] = total
        for o in offsets:
            push(a, o).start()

        @pl.when(jnp.logical_not(single))
        def _():
            for o in offsets:
                tpush(a, o).start()

        re, im = total[0], total[1]
        a2[a, 0, :, 0:order] = re
        a2[a, 0, :, order:2 * order] = -im
        a2[a, 1, :, 0:order] = im
        a2[a, 1, :, order:2 * order] = re

    def stage_c(a, offsets):
        @pl.when(single)
        def _():
            for o in offsets:
                remote(
                    mine.at[a], tbuf.at[a, xoff(o)], tpush_send.at[a, o],
                    t_recv.at[a, xoff(o)], other,
                ).wait_recv()
                t_across(a, o).start()
                wait_block(0, a, xoff(o), ylo)
                move(0, 0, a, xoff(o), ylo, relay_send, o, partner).start()

        @pl.when(jnp.logical_not(single))
        def _():
            for o in offsets:
                wait_block(0, a, xoff(o), ylo)
                move(0, 1, a, xoff(o), ylo, relay2_send, o, across).start()
                move(0, 0, a, xoff(o), ylo, relay_send, o, partner).start()

    def stage_d(a, offsets):
        @pl.when(single)
        def _():
            for o in offsets:
                wait_block(2, a, xoff(o), 1 - ylo)
                move(2, 2, a, xoff(o), 1 - ylo, relay_send, NX + o, partner).start()
                if a != yfirst:
                    move(2, 2, a, xoff(o), 1 - ylo, core_send, o, other).start()

        @pl.when(jnp.logical_not(single))
        def _():
            for o in offsets:
                wait_block(0, a, xoff(o), 1 - ylo)
                move(0, 1, a, xoff(o), 1 - ylo, relay_send, NX + o, across).start()
                if a != yfirst:
                    wait_block(1, a, xoff(o), 1 - ylo)
                    move(1, 1, a, xoff(o), 1 - ylo, core_send, o, other).start()

    def stage_e(a):
        for o in order_x:
            wait_block(role, a, xoff(o), ylo)
            move(role, role, a, xoff(o), ylo, core_send, NX + o, other).start()

    def stage_ew(a):
        @pl.when(single)
        def _():
            for o in range(NX):
                wait_block(0, a, o, 1 - ylo)
        for i in range(NSEC):
            wait_block(3 - role, a, i // 2, i % 2)


    def quarter(p, xx):
        return bbuf.at[p, yfirst, :, pl.ds(pl.multiple_of(xx * wide, wide), wide), :]

    def quarter_part(p, xx, ri):
        return bbuf.at[p, yfirst, ri, pl.ds(pl.multiple_of(xx * wide, wide), wide), :]

    def row_copy(kind, d):
        p = role if kind else 0
        return remote(
            quarter(p, x), quarter(p, x), row_send.at[kind, d], row_recv.at[kind, d], toward[d]
        )

    def row_wait(kind, d):
        p = role if kind else 0
        remote(
            quarter(p, near[1 - d]), quarter(p, near[1 - d]),
            row_send.at[kind, d], row_recv.at[kind, d], toward[d],
        ).wait_recv()

    def row_relay(kind, d):
        p = role if kind else 0
        return remote(
            quarter_part(p, near[1 - d], d), quarter_part(p, near[1 - d], d),
            row_send.at[kind, 2 + d], row_recv.at[kind, 2 + d], toward[d],
        )

    def relay_wait(kind, d):
        p = role if kind else 0
        remote(
            quarter_part(p, xoff(2), d), quarter_part(p, xoff(2), d),
            row_send.at[kind, 2 + d], row_recv.at[kind, 2 + d], toward[d],
        ).wait_recv()

    def pair_copy(p, o):
        return remote(
            quarter(p, xoff(o)), quarter(p, xoff(o)), pair_send.at[o], pair_recv.at[o], other
        )

    def stage_g():
        @pl.when(single)
        def _():
            wait_block(0, yfirst, x, 1 - ylo)
        for d in range(2):
            row_copy(0, d).start()

    def stage_gr():
        @pl.when(jnp.logical_not(single))
        def _():
            wait_block(1, yfirst, x, 1 - ylo)
        wait_block(role, yfirst, x, ylo)
        for d in range(2):
            row_copy(1, d).start()
        pair_copy(role, 0).start()

    def stage_h(kind):
        for d in range(2):
            row_wait(kind, d)
            row_relay(kind, d).start()
            if kind:
                pair_copy(role, 3 - 2 * d).start()

    def stage_i():
        for kind in range(2):
            for d in range(2):
                relay_wait(kind, d)
        pair_copy(role, 2).start()

    def stage_j():
        for o in order_x:
            pair_copy(3 - role, o).wait_recv()

    places = (2 * (1 - c), yhi + c, c + 1 - yhi)
    scale = 0.5 * order ** -0.5

    def out_copy(p, b):
        return pltpu.make_async_copy(
            outb.at[p, b], out_hbm.at[places[p], :, b], out_sem.at[p, b]
        )

    def stage_f(b):
        for p in range(3):
            lhs = a2[...].reshape(n_src * 2 * blk, 2 * order)
            rhs = bbuf[p, b].reshape(2 * order, order)
            res = jnp.dot(lhs, rhs, preferred_element_type=F32) * scale
            outb[p, b] = res.astype(BF).reshape(n_src, 2, blk, order)
            out_copy(p, b).start()

    multiply(0, True)
    multiply(1, True)
    stage_a(0)
    multiply(2, False)
    stage_r(1)
    scatter(2)
    stage_b(0, (0,))
    stage_a(1)
    stage_c(0, (0,))
    stage_r(2)
    stage_b(1, order_x)
    stage_d(0, (0,))
    stage_a(2)
    stage_c(1, (0,))
    stage_b(2, order_x)
    stage_g()
    stage_c(1, (1, 3))
    stage_c(2, (0,))
    stage_c(1, (2,))
    stage_gr()
    stage_d(1, (0, 1))
    stage_c(2, (1, 3))
    stage_d(1, (3, 2))
    stage_h(0)
    stage_c(2, (2,))
    stage_h(1)
    stage_d(2, (0, 1))
    stage_e(1)
    stage_d(2, (3, 2))
    stage_ew(1)
    stage_i()
    stage_f(1)
    stage_e(2)
    stage_j()
    stage_f(0)
    stage_ew(2)
    stage_f(2)

    for a in range(n_src):
        y_copy(a).wait_send()
        for p in range(3):
            out_copy(p, a).wait()
        for d in range(2):
            far_copy(a, d).wait_send()
            for h in range(2):
                near_copy(a, d, h).wait_send()

        def drain(o):
            push(a, o).wait_send()
            move(0, 0, a, xoff(o), ylo, relay_send, o, partner).wait_send()
            move(0, 0, a, xoff(o), ylo, relay2_send, o, across).wait_send()
            move(0, 0, a, xoff(o), ylo, relay_send, NX + o, partner).wait_send()
            if a != yfirst:
                move(0, 0, a, xoff(o), ylo, core_send, o, other).wait_send()
                move(0, 0, a, xoff(o), ylo, core_send, NX + o, other).wait_send()

            @pl.when(jnp.logical_not(single))
            def _():
                tpush(a, o).wait_send()

        for o in range(1 if a == yfirst else NX):
            drain(o)
    for kind in range(2):
        for d in range(2):
            row_copy(kind, d).wait_send()
            row_relay(kind, d).wait_send()
    for o in range(NX):
        pair_copy(role, o).wait_send()


def fused(n_ta, sink, prop, live, times):
    n_src, _, rows, order = prop.shape
    blk, wide = order // NSEC, order // NX
    dma = pltpu.SemaphoreType.DMA
    return pl.pallas_call(
        functools.partial(kernel, n_ta),
        out_shape=jax.ShapeDtypeStruct((3, n_src, n_src, 2, blk, order), BF),
        in_specs=[pl.BlockSpec(memory_space=pltpu.SMEM)] * 2
        + [pl.BlockSpec(memory_space=pl.ANY)] * 2,
        out_specs=pl.BlockSpec(memory_space=pl.ANY),
        scratch_shapes=[
            pltpu.VMEM((2, rows, order), BF),
            pltpu.VMEM((n_src, 2, rows, order), BF),
            pltpu.VMEM((NX, 2, wide, 2 * rows), BF),
            pltpu.VMEM((n_src, NX, 2, wide, order), BF),
            pltpu.VMEM((n_src, 2, 2, blk, order), BF),
            pltpu.VMEM((n_src, 2, 2, wide, order), BF),
            pltpu.VMEM((n_src, 2, blk, order), BF),
            pltpu.VMEM((n_src, 2, blk, order), BF),
            pltpu.VMEM((n_src, 2, blk, order), F32),
            pltpu.VMEM((n_src, 2, blk, order), BF),
            pltpu.VMEM((n_src, 2, blk, 2 * order), BF),
            pltpu.VMEM((3, n_src, 2, order, order), BF),
            pltpu.VMEM((n_src, NX, 2, blk, order), BF),
            pltpu.VMEM((3, n_src, n_src, 2, blk, order), BF),
            dma((1 + n_src,)),
            dma((3, n_src)),
            dma((n_src, 2)),
            dma((n_src, 2)),
            dma((n_src, 2, 2)),
            dma((n_src, 2, 2)),
            dma((n_src,)),
            dma((n_src,)),
            dma((n_src, NX)),
            dma((n_src, NX)),
            dma((3, n_src, NSEC)),
            dma((n_src, NX)),
            dma((n_src, 2 * NX)),
            dma((n_src, NX)),
            dma((n_src, 2 * NX)),
            dma((2, 4)),
            dma((2, 4)),
            dma((NX,)),
            dma((NX,)),
        ],
        compiler_params=pltpu.CompilerParams(
            collective_id=0, has_side_effects=True, vmem_limit_bytes=48 * 1024 * 1024
        ),
        cost_estimate=pl.CostEstimate(
            flops=10_000_000_000, bytes_accessed=12_000_000, transcendentals=0
        ),
    )(live, times, sink, prop)


def solution(mesh):
    n_ta = mesh.shape["ta"]

    def local(sink_vectors, propagators, live_rows, source_times):
        res = fused(n_ta, sink_vectors[:, 0], propagators[:, :, 0], live_rows, source_times)
        return res[:, :, :, :, None]

    return jax.shard_map(
        local,
        mesh=mesh,
        in_specs=(P(None, "ta", "sec", None), P(None, None, "ta", "sec", None), P(), P()),
        out_specs=P(None, None, None, None, "ta", "sec", None),
        check_vma=False,
    )
```
